32 devices in a mesh: dp: 16 (over z, y, x), tensor: 2 (over core).
Axes of the slice: x: 2, y: 2, z: 4, core: 2. Of those that a mesh axis runs over, the one named last changes fastest.
Arguments:
- x_in: bfloat16 [8192, 768], P('dp'), may hold values from -8 to 8
- cotangent: bfloat16 [8192, 768], P('dp'), may hold values from -8 to 8
- norm_gain: float32 [768], replicated, may hold values from 0.5 to 1.5
- w_z: bfloat16 [768, 1536], P(None, 'tensor'), may hold values from -0.21875 to 0.21875
- w_x: bfloat16 [768, 1536], P(None, 'tensor'), may hold values from -0.21875 to 0.21875
- w_bc: bfloat16 [768, 256], replicated, may hold values from -0.21875 to 0.21875
- w_dt: bfloat16 [768, 24], P(None, 'tensor'), may hold values from -0.21875 to 0.21875
- conv_x: float32 [4, 1536], P(None, 'tensor'), may hold values from -3 to 3
- conv_x_bias: float32 [1536], P('tensor'), may hold values from -1.75 to 1.75
- conv_bc: float32 [4, 256], replicated, may hold values from -3 to 3
- conv_bc_bias: float32 [256], replicated, may hold values from -1.75 to 1.75
- dt_bias: float32 [24], P('tensor'), may hold values from -6 to -2
- a_log: float32 [24], P('tensor'), may hold values from 0 to 2.77
- d_skip: float32 [24], P('tensor'), may hold values from 0.5 to 1.5
- gate_norm: float32 [1536], P('tensor'), may hold values from 0.5 to 1.5
- w_out: bfloat16 [1536, 768], P('tensor'), may hold values from -0.3125 to 0.3125
Outputs:
- y_out: bfloat16 [8192, 768], P('dp', 'tensor')
- x_grad: bfloat16 [8192, 768], P('dp', 'tensor')
- norm_gain_grad: float32 [768], P('tensor')
- w_z_grad: float32 [768, 1536], P('dp', 'tensor')
- w_x_grad: float32 [768, 1536], P('dp', 'tensor')
- w_bc_grad: float32 [768, 256], P('dp')
- w_dt_grad: float32 [768, 24], P('dp', 'tensor')
- conv_x_grad: float32 [4, 1536], P(None, 'tensor')
- conv_x_bias_grad: float32 [1536], P('tensor')
- conv_bc_grad: float32 [4, 256], replicated
- conv_bc_bias_grad: float32 [256], replicated
- dt_bias_grad: float32 [24], P('tensor')
- a_log_grad: float32 [24], P('tensor')
- d_skip_grad: float32 [24], P('tensor')
- gate_norm_grad: float32 [1536], P('tensor')
- w_out_grad: float32 [1536, 768], P('tensor', 'dp')
The draws below stay inside these ranges and needn't reach their ends.
All inputs are finite; a program needn't handle non-finite values.
Results may differ from the reference program's by a relative error of at most 0.012.
Values sent between devices are 32-bit elements; how exact they have to be, the bound alone decides.
A program may use at most 128 MiB of HBM per device.

```python
import jax
import jax.numpy as jnp
from jax import lax

D = 768
HEADS = 24
HEAD_DIM = 64
STATE = 128
CONV = 4
GROUP = 256
SEQ_LEN = 512
DI = 1536
TOKENS = 8192


def with_spikes(values, key, source, target, shards_of, factor):
    owner, partner = [(jnp.arange(values.shape[position]) // (values.shape[position] // shards_of)).reshape([-1 if axis == position else 1 for axis in range(values.ndim)]) for position in (source, target)]
    chosen = jax.random.permutation(key, shards_of)[partner]
    strong = (owner == chosen) | (owner == (partner + shards_of // 2) % shards_of)
    return jnp.where(strong, factor * values, values)


def shard_levels(key, extent, cuts, low, high):
    gain, own = 1.0, jax.random.fold_in(key, 6)
    for axis_at, blocks in cuts:
        draws = jnp.exp(jax.random.uniform(jax.random.fold_in(own, axis_at), (blocks,), jnp.float32, low / len(cuts), high / len(cuts)))
        gain = gain * jnp.repeat(draws, extent[axis_at] // blocks).reshape([-1 if axis == axis_at else 1 for axis in range(len(extent))])
    return gain


def centred(rng, extent, width, bound, shards=(), dtype=jnp.bfloat16):
    gain = shard_levels(rng, extent, shards, -0.22, 0.18) if shards else 1.0
    values = jax.random.normal(rng, extent, jnp.float32) * width * gain
    return jnp.minimum(jnp.maximum(values, -bound), bound).astype(dtype)


def gaussian_with(own_key, dims, deviation, bound, cuts, heavy, kind=jnp.bfloat16):
    values = deviation * jax.random.normal(own_key, dims, jnp.float32)
    if cuts:
        values = values * shard_levels(own_key, dims, cuts, -0.22, 0.18)
    return jnp.clip(with_spikes(values, jax.random.fold_in(own_key, 3), *heavy), -bound, bound).astype(kind)


def setup_inputs(seed: int = 0) -> dict:
    splits = jax.random.split(jax.random.key(seed), 17)
    return {
        "x_in": gaussian_with(splits[0], (TOKENS, D), 1.0, 8.0, ((0, 16),), (0, 1, 16, 2.0)),
        "cotangent": gaussian_with(splits[1], (TOKENS, D), 1.0, 8.0, ((0, 16),), (0, 1, 16, 2.0)),
        "norm_gain": jnp.clip(1.0 + 0.1 * jax.random.normal(splits[2], (D,), jnp.float32), 0.5, 1.5),
        "w_z": centred(splits[3], (D, DI), D ** -0.5, 0.21875, ((1, 2),)),
        "w_x": centred(splits[4], (D, DI), D ** -0.5, 0.21875, ((1, 2),)),
        "w_bc": centred(splits[5], (D, 2 * STATE), D ** -0.5, 0.21875),
        "w_dt": centred(splits[6], (D, HEADS), D ** -0.5, 0.21875, ((1, 2),)),
        "conv_x": centred(splits[7], (CONV, DI), CONV ** -0.5, 3.0, ((1, 2),), jnp.float32),
        "conv_x_bias": centred(splits[8], (DI,), 0.3, 1.75, ((0, 2),), jnp.float32),
        "conv_bc": centred(splits[9], (CONV, 2 * STATE), CONV ** -0.5, 3.0, (), jnp.float32),
        "conv_bc_bias": centred(splits[10], (2 * STATE,), 0.3, 1.75, (), jnp.float32),
        "dt_bias": jnp.clip(-6.0 + 4.0 * jax.random.uniform(splits[11], (HEADS,), jnp.float32) ** shard_levels(splits[11], (HEADS,), ((0, 2),), -0.2, 0.2), -6.0, -2.0),
        "a_log": jnp.clip(2.77 * jax.random.uniform(splits[12], (HEADS,), jnp.float32) ** shard_levels(splits[12], (HEADS,), ((0, 2),), -0.2, 0.2), 0.0, 2.77),
        "d_skip": jnp.clip(0.5 + 1.0 * jax.random.uniform(splits[13], (HEADS,), jnp.float32) ** shard_levels(splits[13], (HEADS,), ((0, 2),), -0.2, 0.2), 0.5, 1.5),
        "gate_norm": jnp.clip(1.0 + 0.1 * jax.random.normal(splits[14], (DI,), jnp.float32), 0.5, 1.5),
        "w_out": centred(splits[15], (DI, D), (DI // 4) ** -0.5, 0.3125, ((0, 2),)),
    }


epsilon = 1e-05
precise = lax.Precision.HIGHEST

@jax.custom_vjp
def low(v):
    return lax.optimization_barrier(v.astype(jnp.bfloat16)).astype(jnp.float32)

@jax.custom_vjp
def low_back(v):
    return v

def low_keep(v):
    return (low(v), None)

def low_pass(kept, grad):
    return (grad,)

def back_keep(v):
    return (v, None)

def back_low(kept, grad):
    return (low(grad),)
low.defvjp(low_keep, low_pass)
low_back.defvjp(back_keep, back_low)

def causal_conv(pre_conv, kernel, offset):
    taps = kernel.shape[0]
    padded = jnp.pad(pre_conv, ((taps - 1, 0), (0, 0)))
    summed = offset[None, :] + kernel[0][None, :] * padded[:pre_conv.shape[0]]
    for tap_index in range(1, taps):
        summed = summed + kernel[tap_index][None, :] * padded[tap_index:tap_index + pre_conv.shape[0]]
    return summed

def block_pass(carry_state, piece_in):
    values, b_rows, c_rows, decay_log, step_size = piece_in
    length = values.shape[0]
    running = jnp.cumsum(decay_log, axis=0)
    causal = jnp.arange(length)[:, None] >= jnp.arange(length)[None, :]
    differ = jnp.where(causal[:, :, None], running[:, None, :] - running[None, :, :], -jnp.inf)
    pair_dot = jnp.einsum('in,jn->ij', c_rows, b_rows, precision=precise)
    weights = pair_dot[:, :, None] * jnp.exp(differ) * step_size[None, :, :]
    within = jnp.einsum('ijh,jhp->ihp', weights, values, precision=precise)
    carried = jnp.einsum('in,hpn->ihp', c_rows, carry_state, precision=precise) * jnp.exp(running)[:, :, None]
    to_end = jnp.exp(running[-1][None, :] - running) * step_size
    state_next = carry_state * jnp.exp(running[-1])[:, None, None] + jnp.einsum('jhp,jn->hpn', to_end[:, :, None] * values, b_rows, precision=precise)
    return (state_next, within + carried)

def scan_sequence(values, b_rows, c_rows, step_size, decay_rate):
    length, heads, head_width = values.shape
    blocks = length // GROUP

    def split_rows(array):
        return array.reshape((blocks, GROUP) + array.shape[1:])
    decay_log = step_size * decay_rate[None, :]
    start = jnp.zeros((heads, head_width, b_rows.shape[1]), jnp.float32)
    outputs = lax.scan(jax.checkpoint(block_pass), start, (split_rows(values), split_rows(b_rows), split_rows(c_rows), split_rows(decay_log), split_rows(step_size)))[1]
    return outputs.reshape(values.shape)

def layer_forward(tokens, params):
    norm_gain, w_z, w_x, w_bc, w_dt, conv_x, conv_x_bias, conv_bc, conv_bc_bias, dt_bias, a_log, d_skip, gate_norm, w_out = params
    inv_rms = lax.rsqrt(lax.optimization_barrier(jnp.mean(tokens * tokens, axis=1, keepdims=True)) + epsilon)
    normed = low(tokens * inv_rms * norm_gain[None, :])
    gate_pre = low_back(jnp.dot(normed, w_z, precision=precise))
    x_pre = low_back(jnp.dot(normed, w_x, precision=precise))
    bc_pre = low_back(jnp.dot(normed, w_bc, precision=precise))
    dt_pre = low_back(jnp.dot(normed, w_dt, precision=precise))
    x_conv = low(jax.nn.silu(causal_conv(x_pre, conv_x, conv_x_bias)))
    bc_conv = low(jax.nn.silu(causal_conv(bc_pre, conv_bc, conv_bc_bias)))
    step_size = jax.nn.softplus(dt_pre + dt_bias[None, :])
    decay_rate = -jnp.exp(a_log)
    length = tokens.shape[0]
    values = x_conv.reshape(length, HEADS, HEAD_DIM)
    scanned = scan_sequence(values, bc_conv[:, :STATE], bc_conv[:, STATE:], step_size, decay_rate)
    mixed_out = (scanned + d_skip[None, :, None] * values).reshape(length, -1)
    gated_vals = mixed_out * jax.nn.silu(gate_pre)
    spread = lax.rsqrt(lax.optimization_barrier(jnp.mean(gated_vals * gated_vals, axis=1, keepdims=True)) + epsilon)
    gate_out = low(gated_vals * spread * gate_norm[None, :])
    return tokens + jnp.dot(gate_out, w_out, precision=precise)

def reference(x_in, cotangent, norm_gain, w_z, w_x, w_bc, w_dt, conv_x, conv_x_bias, conv_bc, conv_bc_bias, dt_bias, a_log, d_skip, gate_norm, w_out):
    params = tuple((param.astype(jnp.float32) for param in (norm_gain, w_z, w_x, w_bc, w_dt, conv_x, conv_x_bias, conv_bc, conv_bc_bias, dt_bias, a_log, d_skip, gate_norm, w_out)))
    token_seqs = x_in.astype(jnp.float32).reshape(-1, SEQ_LEN, D)
    cot_seqs = cotangent.astype(jnp.float32).reshape(-1, SEQ_LEN, D)

    def one_sequence(totals, pieces):
        tokens, cot_rows = pieces
        result, pullback = jax.vjp(layer_forward, tokens, params)
        token_grad, param_grads = pullback(cot_rows)
        summed = tuple((left + right for left, right in zip(totals, param_grads)))
        return (summed, (result.astype(jnp.bfloat16), token_grad.astype(jnp.bfloat16)))
    totals, outputs = lax.scan(one_sequence, tuple((jnp.zeros_like(param) for param in params)), (token_seqs, cot_seqs))
    return (outputs[0].reshape(-1, D), outputs[1].reshape(-1, D), totals[0], totals[1], totals[2], totals[3], totals[4], totals[5], totals[6], totals[7], totals[8], totals[9], totals[10], totals[11], totals[12], totals[13])
```

```python
import functools

import jax
import jax.numpy as jnp
from jax import lax
from jax.experimental import pallas as pl
from jax.experimental.pallas import tpu as pltpu
from jax.sharding import PartitionSpec as P

GROUP = 256
SEQ_LEN = 512


epsilon = 1e-05
precise = lax.Precision.HIGHEST


def lead_contract(left, right):
    return lax.dot_general(
        left, right, (((0,), (0,)), ((), ())), preferred_element_type=jnp.float32
    )


def tail_contract(left, right):
    return lax.dot_general(
        left, right, (((1,), (1,)), ((), ())), preferred_element_type=jnp.float32
    )


def causal_conv(pre_conv, kernel, offset):
    taps = kernel.shape[0]
    padded = jnp.pad(pre_conv, ((taps - 1, 0), (0, 0)))
    summed = offset[None, :] + kernel[0][None, :] * padded[: pre_conv.shape[0]]
    for tap_index in range(1, taps):
        summed = (
            summed + kernel[tap_index][None, :] * padded[tap_index : tap_index + pre_conv.shape[0]]
        )
    return summed


def block_pass(carry_state, piece_in):
    values, b_rows, c_rows, decay_log, step_size = piece_in
    length = values.shape[0]
    running = jnp.cumsum(decay_log, axis=1)
    causal = jnp.arange(length)[:, None] >= jnp.arange(length)[None, :]
    differ = jnp.where(causal[None, :, :], running[:, :, None] - running[:, None, :], -jnp.inf)
    pair_dot = jnp.einsum(
        "in,jn->ij",
        c_rows.astype(jnp.bfloat16),
        b_rows.astype(jnp.bfloat16),
        preferred_element_type=jnp.float32,
    )
    weights = pair_dot[None, :, :] * jnp.exp(differ) * step_size[:, None, :]
    within = jnp.einsum("hij,jhp->ihp", weights, values, precision=precise)
    carried = (
        jnp.einsum("in,hpn->ihp", c_rows, carry_state, precision=precise)
        * jnp.transpose(jnp.exp(running))[:, :, None]
    )
    to_end = jnp.exp(running[:, -1:] - running) * step_size
    state_next = carry_state * jnp.exp(running[:, -1])[:, None, None] + jnp.einsum(
        "jhp,jn->hpn", jnp.transpose(to_end)[:, :, None] * values, b_rows, precision=precise
    )
    return (state_next, within + carried)


def scan_sequence(values, b_rows, c_rows, step_size, decay_rate):
    length, heads, head_width = values.shape
    blocks = length // GROUP

    def split_rows(array):
        return array.reshape((blocks, GROUP) + array.shape[1:])

    def split_heads(array):
        return jnp.transpose(jnp.transpose(array).reshape(heads, blocks, GROUP), (1, 0, 2))

    decay_log = step_size * decay_rate[None, :]
    start = jnp.zeros((heads, head_width, b_rows.shape[1]), jnp.float32)
    outputs = lax.scan(
        jax.checkpoint(block_pass),
        start,
        (
            split_rows(values),
            split_rows(b_rows),
            split_rows(c_rows),
            split_heads(decay_log),
            split_heads(step_size),
        ),
    )[1]
    return outputs.reshape(values.shape)


PACK_ROWS = 16


def bit_orders(levels):
    if levels == 4:
        return ((0, 1, 2, 3), (1, 0, 2, 3), (2, 3, 0, 1))
    base = tuple(range(levels))
    third = max(1, levels // 3)
    return (base, base[third:] + base[:third], base[2 * third :] + base[: 2 * third])


def reduce_kernel(
    orders, a_ref, b_ref, c_ref, pack_ref, oa_ref, ob_ref, oc_ref, opack_ref,
    ra_ref, rb_ref, rc_ref, rpack_ref, spack_ref, send_sem, recv_sem, psend_sem, precv_sem,
):
    parts, outs, lands = (a_ref, b_ref, c_ref), (oa_ref, ob_ref, oc_ref), (ra_ref, rb_ref, rc_ref)
    levels = len(orders[0])
    count = 2**levels
    sizes = [count // 2 ** (stage + 1) for stage in range(levels)]
    starts = [sum(sizes[:stage]) for stage in range(levels)]
    me = lax.axis_index("dp")

    def my_bit(bit):
        return (me // 2**bit) % 2

    def partner(bit):
        return me + (1 - 2 * my_bit(bit)) * 2**bit

    def first_chunk(order, k, kept):
        own = my_bit(order[0])
        chunk = (own if kept else 1 - own) * 2 ** order[0]
        for place in range(1, levels):
            relative = (k // 2 ** (levels - 1 - place)) % 2
            chunk = chunk + ((my_bit(order[place]) + relative + 1) % 2) * 2 ** order[place]
        return chunk

    def transfer(g, stage, k):
        if stage == 0:
            source = parts[g].at[first_chunk(orders[g], k, False)]
        else:
            source = lands[g].at[starts[stage - 1] + k]
        slot = starts[stage] + k
        return pltpu.make_async_remote_copy(
            src_ref=source,
            dst_ref=lands[g].at[slot],
            send_sem=send_sem.at[g, slot],
            recv_sem=recv_sem.at[g, slot],
            device_id={"dp": partner(orders[g][stage])},
            device_id_type=pl.DeviceIdType.MESH,
        )

    def pack_transfer(stage):
        return pltpu.make_async_remote_copy(
            src_ref=pack_ref if stage == 0 else spack_ref.at[stage - 1],
            dst_ref=rpack_ref.at[stage],
            send_sem=psend_sem.at[stage],
            recv_sem=precv_sem.at[stage],
            device_id={"dp": partner(stage)},
            device_id_type=pl.DeviceIdType.MESH,
        )

    barrier = pltpu.get_barrier_semaphore()
    for bit in range(levels):
        pl.semaphore_signal(
            barrier, inc=1, device_id={"dp": partner(bit)}, device_id_type=pl.DeviceIdType.MESH
        )
    pl.semaphore_wait(barrier, levels)

    def begin(k, carry):
        for g in range(3):
            transfer(g, 0, k).start()
        return carry

    pack_transfer(0).start()
    lax.fori_loop(0, sizes[0], begin, 0)
    for stage in range(levels):
        half = sizes[stage] // 2
        for g in range(3):

            def step(k, carry, g=g, stage=stage, forward=False):
                transfer(g, stage, k).wait_recv()
                slot = starts[stage] + k
                if stage == 0:
                    own = parts[g][first_chunk(orders[g], k, True)]
                else:
                    own = lands[g][starts[stage - 1] + sizes[stage] + k]
                total = lands[g][slot] + own
                if stage == levels - 1:
                    outs[g][...] = total
                else:
                    lands[g][slot] = total
                if forward:
                    transfer(g, stage + 1, k).start()
                return carry

            if stage < levels - 1:
                lax.fori_loop(0, half, functools.partial(step, forward=True), 0)
                lax.fori_loop(half, sizes[stage], step, 0)
            else:
                step(0, 0)
        pack_transfer(stage).wait_recv()
        before = pack_ref[...] if stage == 0 else spack_ref[stage - 1]
        pack_total = before + rpack_ref[stage]
        if stage == levels - 1:
            opack_ref[...] = pack_total
        else:
            spack_ref[stage] = pack_total
            pack_transfer(stage + 1).start()
    for stage in range(levels):
        pack_transfer(stage).wait_send()

        def finish(k, carry, stage=stage):
            for g in range(3):
                transfer(g, stage, k).wait_send()
            return carry

        lax.fori_loop(0, sizes[stage], finish, 0)


def reduce_all(a, b, c, pack):
    count, rows, width = a.shape
    levels = count.bit_length() - 1
    vmem = pl.BlockSpec(memory_space=pltpu.VMEM)
    part = jax.ShapeDtypeStruct((rows, width), jnp.float32)
    return pl.pallas_call(
        functools.partial(reduce_kernel, bit_orders(levels)),
        out_shape=(part, part, part, jax.ShapeDtypeStruct(pack.shape, jnp.float32)),
        in_specs=[vmem] * 4,
        out_specs=(vmem,) * 4,
        scratch_shapes=[pltpu.VMEM((count - 1, rows, width), jnp.float32)] * 3
        + [
            pltpu.VMEM((levels,) + pack.shape, jnp.float32),
            pltpu.VMEM((levels,) + pack.shape, jnp.float32),
            pltpu.SemaphoreType.DMA((3, count - 1)),
            pltpu.SemaphoreType.DMA((3, count - 1)),
            pltpu.SemaphoreType.DMA((levels,)),
            pltpu.SemaphoreType.DMA((levels,)),
        ],
        compiler_params=pltpu.CompilerParams(
            collective_id=0, has_side_effects=True, vmem_limit_bytes=44 * 2**20
        ),
        name="reduce_all",
    )(a, b, c, pack)


def on_device(
    x_in,
    cotangent,
    norm_gain,
    w_z,
    w_x,
    w_bc,
    w_dt,
    conv_x,
    conv_x_bias,
    conv_bc,
    conv_bc_bias,
    dt_bias,
    a_log,
    d_skip,
    gate_norm,
    w_out,
):
    row_count, model_width = x_in.shape
    pair_count = lax.axis_size("tensor")
    half_width = model_width // pair_count
    col_start = lax.axis_index("tensor") * half_width
    inner_width = w_z.shape[1]
    heads_here = dt_bias.shape[0]
    seq_count = row_count // SEQ_LEN
    total_width = inner_width * pair_count
    tokens = x_in.astype(jnp.float32)
    inv_rms = lax.rsqrt(jnp.mean(tokens * tokens, axis=1, keepdims=True) + epsilon)
    x_hat = tokens * inv_rms
    normed = (x_hat * norm_gain[None, :]).astype(jnp.bfloat16)
    gate_pre = jnp.dot(normed, w_z, preferred_element_type=jnp.float32)
    x_pre = jnp.dot(normed, w_x, preferred_element_type=jnp.float32)
    bc_pre = jnp.dot(normed, w_bc, preferred_element_type=jnp.float32)
    dt_pre = jnp.dot(normed, w_dt, preferred_element_type=jnp.float32)

    def conv_piece(x_part, bc_part, kernel_x, offset_x, kernel_bc, offset_bc):
        conv_seq = jax.vmap(causal_conv, (0, None, None))
        x_result = jax.nn.silu(conv_seq(x_part.reshape(seq_count, SEQ_LEN, -1), kernel_x, offset_x))
        bc_result = jax.nn.silu(
            conv_seq(bc_part.reshape(seq_count, SEQ_LEN, -1), kernel_bc, offset_bc)
        )
        return (x_result.reshape(row_count, -1), bc_result.reshape(row_count, -1))

    (x_conv, bc_conv), conv_back = jax.vjp(
        conv_piece, x_pre, bc_pre, conv_x, conv_x_bias, conv_bc, conv_bc_bias
    )
    x_low, bc_low = lax.optimization_barrier(
        (x_conv.astype(jnp.bfloat16), bc_conv.astype(jnp.bfloat16))
    )
    state_width = bc_low.shape[1] // 2

    def mixer_piece(x_vals, bc_vals, dt_vals, dt_offset, decay_log_rate, skip_gain):
        step_size = jax.nn.softplus(dt_vals + dt_offset[None, :])
        decay_rate = -jnp.exp(decay_log_rate)
        values = x_vals.reshape(seq_count, SEQ_LEN, heads_here, -1)
        bc_seq = bc_vals.reshape(seq_count, SEQ_LEN, -1)
        scanned = jax.vmap(scan_sequence, (0, 0, 0, 0, None))(
            values,
            bc_seq[:, :, :state_width],
            bc_seq[:, :, state_width:],
            step_size.reshape(seq_count, SEQ_LEN, heads_here),
            decay_rate,
        )
        return (scanned + skip_gain[None, None, :, None] * values).reshape(row_count, -1)

    mixed_out, mixer_back = jax.vjp(
        mixer_piece,
        x_low.astype(jnp.float32),
        bc_low.astype(jnp.float32),
        dt_pre,
        dt_bias,
        a_log,
        d_skip,
    )
    gate_act = jax.nn.silu(gate_pre)
    gated_vals = mixed_out * gate_act
    square_sum = lax.psum(jnp.sum(gated_vals * gated_vals, axis=1), "tensor")
    spread = lax.rsqrt(square_sum / total_width + epsilon)[:, None]
    gate_out = (gated_vals * spread * gate_norm[None, :]).astype(jnp.bfloat16)
    out_share = lax.psum_scatter(
        jnp.dot(gate_out, w_out, preferred_element_type=jnp.float32),
        "tensor",
        scatter_dimension=1,
        tiled=True,
    )
    token_half = lax.dynamic_slice_in_dim(tokens, col_start, half_width, 1)
    result = (token_half + out_share).astype(jnp.bfloat16)
    out_grad = tail_contract(cotangent, w_out)
    w_out_grad = lead_contract(cotangent, gate_out)
    gate_norm_grad = jnp.sum(out_grad * gated_vals * spread, axis=0)
    weighted = out_grad * gate_norm[None, :]
    row_dot = lax.psum(jnp.sum(weighted * gated_vals, axis=1), "tensor")
    gated_grad = spread * weighted - gated_vals * spread**3 * row_dot[:, None] / total_width
    sigma = jax.nn.sigmoid(gate_pre)
    mixed_grad = gated_grad * gate_act
    gate_low = (gated_grad * mixed_out * sigma * (1.0 + gate_pre * (1.0 - sigma))).astype(
        jnp.bfloat16
    )
    x_conv_grad, bc_part_grad, dt_grad, dt_bias_grad, a_log_grad, d_skip_grad = mixer_back(
        mixed_grad
    )
    bc_conv_grad = lax.psum(bc_part_grad, "tensor")
    x_pre_grad, bc_pre_grad, conv_x_grad, conv_x_bias_grad, conv_bc_grad, conv_bc_bias_grad = (
        conv_back((x_conv_grad, bc_conv_grad))
    )
    x_pre_low = x_pre_grad.astype(jnp.bfloat16)
    bc_pre_low = bc_pre_grad.astype(jnp.bfloat16)
    dt_low = dt_grad.astype(jnp.bfloat16)
    partial_grad = (
        tail_contract(gate_low, w_z) + tail_contract(x_pre_low, w_x) + tail_contract(dt_low, w_dt)
    )
    hat_half = lax.dynamic_slice_in_dim(x_hat, col_start, half_width, 1)
    gain_half = lax.dynamic_slice_in_dim(norm_gain, col_start, half_width, 0)
    normed_grad = lax.psum(partial_grad, "tensor") + tail_contract(bc_pre_low, w_bc)
    grad_half = lax.dynamic_slice_in_dim(normed_grad, col_start, half_width, 1)
    weighted_in = grad_half * gain_half[None, :]
    in_dot = jnp.sum(normed_grad * norm_gain[None, :] * x_hat, axis=1)
    norm_gain_grad = jnp.sum(grad_half * hat_half, axis=0)
    cot_half = lax.dynamic_slice_in_dim(cotangent, col_start, half_width, 1).astype(jnp.float32)
    x_grad = (cot_half + inv_rms * (weighted_in - hat_half * in_dot[:, None] / model_width)).astype(
        jnp.bfloat16
    )
    count = lax.axis_size("dp")
    half_bc = bc_pre_low.shape[1] // 2
    dt_padded = jnp.pad(dt_low, ((0, 0), (0, half_bc - heads_here)))

    def chunks(array):
        return array.reshape(count, model_width // count, array.shape[1])

    part_a = chunks(jnp.concatenate([w_out_grad, lead_contract(normed, dt_padded)], axis=1))
    part_b = chunks(
        lead_contract(normed, jnp.concatenate([gate_low, bc_pre_low[:, :half_bc]], axis=1))
    )
    part_c = chunks(
        lead_contract(normed, jnp.concatenate([x_pre_low, bc_pre_low[:, half_bc:]], axis=1))
    )
    small = (
        conv_x_grad,
        conv_x_bias_grad,
        conv_bc_grad,
        conv_bc_bias_grad,
        dt_bias_grad,
        a_log_grad,
        d_skip_grad,
        gate_norm_grad,
        norm_gain_grad,
    )
    flat = jnp.concatenate([array.reshape(-1) for array in small])
    pack = jnp.pad(flat, (0, PACK_ROWS * 768 - flat.shape[0])).reshape(PACK_ROWS, 768)
    sum_a, sum_b, sum_c, pack_total = reduce_all(part_a, part_b, part_c, pack)
    w_out_share = jnp.transpose(sum_a[:, :inner_width])
    w_dt_share = sum_a[:, inner_width : inner_width + heads_here]
    w_z_share = sum_b[:, :inner_width]
    w_x_share = sum_c[:, :inner_width]
    w_bc_share = jnp.concatenate([sum_b[:, inner_width:], sum_c[:, inner_width:]], axis=1)
    flat_total = pack_total.reshape(-1)
    totals, at = [], 0
    for array in small:
        totals.append(flat_total[at : at + array.size].reshape(array.shape))
        at += array.size
    (
        conv_x_total,
        conv_x_bias_total,
        conv_bc_total,
        conv_bc_bias_total,
        dt_bias_total,
        a_log_total,
        d_skip_total,
        gate_norm_total,
        norm_gain_total,
    ) = totals
    return (
        result,
        x_grad,
        norm_gain_total,
        w_z_share,
        w_x_share,
        w_bc_share,
        w_dt_share,
        conv_x_total,
        conv_x_bias_total,
        conv_bc_total,
        conv_bc_bias_total,
        dt_bias_total,
        a_log_total,
        d_skip_total,
        gate_norm_total,
        w_out_share,
    )


def solution(mesh):
    in_specs = (
        P("dp", None),
        P("dp", None),
        P(),
        P(None, "tensor"),
        P(None, "tensor"),
        P(),
        P(None, "tensor"),
        P(None, "tensor"),
        P("tensor"),
        P(),
        P(),
        P("tensor"),
        P("tensor"),
        P("tensor"),
        P("tensor"),
        P("tensor", None),
    )
    out_specs = (
        P("dp", "tensor"),
        P("dp", "tensor"),
        P("tensor"),
        P("dp", "tensor"),
        P("dp", "tensor"),
        P("dp", None),
        P("dp", "tensor"),
        P(None, "tensor"),
        P("tensor"),
        P(),
        P(),
        P("tensor"),
        P("tensor"),
        P("tensor"),
        P("tensor"),
        P("tensor", "dp"),
    )
    return jax.shard_map(
        on_device, mesh=mesh, in_specs=in_specs, out_specs=out_specs, check_vma=False
    )
```

```python
import functools

import jax
import jax.numpy as jnp
from jax import lax
from jax.experimental import pallas as pl
from jax.experimental.pallas import tpu as pltpu
from jax.sharding import PartitionSpec as P

GROUP = 256


epsilon = 1e-05
precise = lax.Precision.HIGHEST


def lead_contract(left, right):
    return lax.dot_general(
        left, right, (((0,), (0,)), ((), ())), preferred_element_type=jnp.float32
    )


def tail_contract(left, right):
    return lax.dot_general(
        left, right, (((1,), (1,)), ((), ())), preferred_element_type=jnp.float32
    )


def causal_conv(pre_conv, kernel, offset):
    taps = kernel.shape[0]
    padded = jnp.pad(pre_conv, ((taps - 1, 0), (0, 0)))
    summed = offset[None, :] + kernel[0][None, :] * padded[: pre_conv.shape[0]]
    for tap_index in range(1, taps):
        summed = (
            summed + kernel[tap_index][None, :] * padded[tap_index : tap_index + pre_conv.shape[0]]
        )
    return summed


LANES = 128


def low_dot(left, right, contract):
    return lax.dot_general(
        left.astype(jnp.bfloat16),
        right.astype(jnp.bfloat16),
        ((contract[0], contract[1]), ((), ())),
        preferred_element_type=jnp.float32,
    )


PLAIN, LEAD, TAIL = ((1,), (0,)), ((0,), (0,)), ((1,), (1,))


def shifted(rows, distance):
    if distance == 0:
        return rows
    length = rows.shape[0]
    at = lax.broadcasted_iota(jnp.int32, rows.shape, 0)
    moved = pltpu.roll(rows, distance % length, 0)
    keep = at >= distance if distance > 0 else at < length + distance
    return jnp.where(keep, moved, 0.0)


def conv_rows(pre, taps, offset):
    count = taps.shape[0]
    total = offset + taps[count - 1 : count] * pre
    for k in range(count - 1):
        total = total + taps[k : k + 1] * shifted(pre, count - 1 - k)
    return total


def pick(array, head):
    lane = lax.broadcasted_iota(jnp.int32, array.shape, 1)
    return jnp.sum(jnp.where(lane == head, array, 0.0), axis=1, keepdims=True)


def lower(size):
    return lax.broadcasted_iota(jnp.int32, (size, size), 0) >= lax.broadcasted_iota(
        jnp.int32, (size, size), 1
    )


def prepare(dt_ref, dtb_ref, alog_ref, bc_ref, cbc_ref, cbcb_ref, scratch):
    step_ref, run_ref, stept_ref, runt_ref, bc_low_ref, pair_ref = scratch
    step = dt_ref[...] + dtb_ref[...]
    step = jnp.maximum(step, 0.0) + jnp.log1p(jnp.exp(-jnp.abs(step)))
    step_ref[...] = step
    decay = step * -jnp.exp(alog_ref[...])
    u = conv_rows(bc_ref[...], cbc_ref[...], cbcb_ref[...])
    bc_low_ref[...] = (u * jax.nn.sigmoid(u)).astype(jnp.bfloat16)
    state = bc_low_ref.shape[1] // 2
    tri = lower(GROUP).astype(jnp.float32)
    for block in range(2):
        rows = slice(block * GROUP, (block + 1) * GROUP)
        run = jnp.dot(tri, decay[rows], precision=precise, preferred_element_type=jnp.float32)
        run_ref[rows, :] = run
        runt_ref[:, rows] = run.T
        stept_ref[:, rows] = step[rows].T
        pair_ref[block] = low_dot(bc_low_ref[rows, state:], bc_low_ref[rows, :state], TAIL)


def prepare_scratch(rows, width):
    return [
        pltpu.VMEM((rows, LANES), jnp.float32),
        pltpu.VMEM((rows, LANES), jnp.float32),
        pltpu.VMEM((LANES, rows), jnp.float32),
        pltpu.VMEM((LANES, rows), jnp.float32),
        pltpu.VMEM((rows, width), jnp.bfloat16),
        pltpu.VMEM((2, GROUP, GROUP), jnp.float32),
    ]


def forward_kernel(
    x_ref, cot_ref, gain_ref, wz_ref, wx_ref, wbc_ref, wdt_ref, cx_ref, cxb_ref, cbc_ref, cbcb_ref,
    dtb_ref, alog_ref, skip_ref, gnorm_ref, wout_ref,
    normed_ref, gate_ref, xpre_ref, bc_ref, dt_ref, mixed_ref, og_ref, state_ref, sums_ref,
    *scratch,
):
    step_ref, run_ref, stept_ref, runt_ref, bc_low_ref, pair_ref = scratch
    tokens = x_ref[...].astype(jnp.float32)
    inv_rms = lax.rsqrt(jnp.mean(tokens * tokens, axis=1, keepdims=True) + epsilon)
    normed_ref[...] = (tokens * inv_rms * gain_ref[...]).astype(jnp.bfloat16)
    bc_ref[...] = low_dot(normed_ref[...], wbc_ref[...], PLAIN)
    dt_ref[...] = low_dot(normed_ref[...], wdt_ref[...], PLAIN)
    prepare(dt_ref, dtb_ref, alog_ref, bc_ref, cbc_ref, cbcb_ref, scratch)
    sums_ref[...] = jnp.zeros_like(sums_ref)
    state = bc_low_ref.shape[1] // 2
    lane = lax.broadcasted_iota(jnp.int32, (1, LANES), 1)
    left = lane < LANES // 2

    def pair_step(p, carry):
        cols = pl.ds(pl.multiple_of(p * LANES, LANES), LANES)
        pre = low_dot(normed_ref[...], wx_ref[:, cols], PLAIN)
        xpre_ref[:, cols] = pre
        gate = low_dot(normed_ref[...], wz_ref[:, cols], PLAIN)
        gate_ref[:, cols] = gate
        u = conv_rows(pre, cx_ref[:, cols], cxb_ref[:, cols])
        x_low = (u * jax.nn.sigmoid(u)).astype(jnp.bfloat16)
        values = x_low.astype(jnp.float32)
        carried_state = None
        for block in range(2):
            rows = slice(block * GROUP, (block + 1) * GROUP)
            part = values[rows]
            b_rows, c_rows = bc_low_ref[rows, :state], bc_low_ref[rows, state:]
            run_cols = [pick(run_ref[rows, :], 2 * p + side) for side in range(2)]
            total = skip_ref[:, cols] * part
            for side in range(2):
                run_row = runt_ref[pl.ds(2 * p + side, 1), rows]
                step_row = stept_ref[pl.ds(2 * p + side, 1), rows]
                differ = jnp.where(lower(GROUP), run_cols[side] - run_row, -jnp.inf)
                weights = pair_ref[block] * jnp.exp(differ) * step_row
                mine = left if side == 0 else ~left
                total = total + low_dot(weights, jnp.where(mine, part, 0.0), PLAIN)
            run = jnp.where(left, run_cols[0], run_cols[1])
            if block == 0:
                step = jnp.where(
                    left, pick(step_ref[rows, :], 2 * p), pick(step_ref[rows, :], 2 * p + 1)
                )
                to_end = jnp.exp(run[GROUP - 1 :] - run) * step
                carried_state = low_dot(to_end * part, b_rows, LEAD)
                state_ref[cols, :] = carried_state
            else:
                total = total + jnp.exp(run) * low_dot(c_rows, carried_state, TAIL)
            mixed_ref[rows, cols] = total
        gated = mixed_ref[:, cols] * gate * jax.nn.sigmoid(gate)
        og = low_dot(cot_ref[...], wout_ref[cols, :], TAIL)
        og_ref[:, cols] = og
        square = jnp.sum(gated * gated, axis=1, keepdims=True)
        inner = jnp.sum(og * gnorm_ref[:, cols] * gated, axis=1, keepdims=True)
        sums_ref[...] += jnp.where(lane == 0, square, 0.0) + jnp.where(lane == 1, inner, 0.0)
        return carry

    lax.fori_loop(0, gate_ref.shape[1] // LANES, pair_step, 0)


def backward_kernel(
    total_width,
    sums_ref, gate_ref, xpre_ref, bc_ref, dt_ref, mixed_ref, og_ref, state_ref,
    wz_ref, wx_ref, wdt_ref, cx_ref, cxb_ref, cbc_ref, cbcb_ref, dtb_ref, alog_ref, skip_ref,
    gnorm_ref, wout_ref,
    gout_ref, y_ref, glow_ref, xlow_ref, dtlow_ref, bcg_ref, partial_ref, rows_ref, heads_ref,
    *scratch,
):
    step_ref, run_ref, stept_ref, runt_ref, bc_low_ref, pair_ref = scratch[:6]
    run_grad_ref, direct_ref, colt_ref, both_ref = scratch[6:]
    prepare(dt_ref, dtb_ref, alog_ref, bc_ref, cbc_ref, cbcb_ref, scratch[:6])
    for ref in (run_grad_ref, direct_ref, colt_ref, both_ref, bcg_ref, rows_ref, heads_ref):
        ref[...] = jnp.zeros_like(ref)
    state = bc_low_ref.shape[1] // 2
    lane = lax.broadcasted_iota(jnp.int32, (1, LANES), 1)
    left = lane < LANES // 2
    taps = cx_ref.shape[0]

    def split_sum(array):
        return (
            jnp.sum(jnp.where(left, array, 0.0), axis=1, keepdims=True),
            jnp.sum(jnp.where(left, 0.0, array), axis=1, keepdims=True),
        )

    def pair_step(p, carry):
        cols = pl.ds(pl.multiple_of(p * LANES, LANES), LANES)
        spread = lax.rsqrt(sums_ref[:, 0:1] / total_width + epsilon)
        row_dot = sums_ref[:, 1:2]
        gate, mixed, og = gate_ref[:, cols], mixed_ref[:, cols], og_ref[:, cols]
        sigma = jax.nn.sigmoid(gate)
        gate_act = gate * sigma
        gated = mixed * gate_act
        gout_ref[:, cols] = (gated * spread * gnorm_ref[:, cols]).astype(jnp.bfloat16)
        rows_ref[5:6, cols] = jnp.sum(og * gated * spread, axis=0, keepdims=True)
        gated_grad = spread * og * gnorm_ref[:, cols] - gated * (
            spread * spread * spread * row_dot / total_width
        )
        grad = gated_grad * gate_act
        glow_ref[:, cols] = (
            gated_grad * mixed * sigma * (1.0 + gate * (1.0 - sigma))
        ).astype(jnp.bfloat16)
        pre = xpre_ref[:, cols]
        u = conv_rows(pre, cx_ref[:, cols], cxb_ref[:, cols])
        act = jax.nn.sigmoid(u)
        values = (u * act).astype(jnp.bfloat16).astype(jnp.float32)
        rows_ref[6:7, cols] = jnp.sum(grad * values, axis=0, keepdims=True)
        kept = state_ref[cols, :]
        later = None
        pieces = [None, None]
        for block in (1, 0):
            rows = slice(block * GROUP, (block + 1) * GROUP)
            part, dy = values[rows], grad[rows]
            b_rows, c_rows = bc_low_ref[rows, :state], bc_low_ref[rows, state:]
            run_cols = [pick(run_ref[rows, :], 2 * p + side) for side in range(2)]
            run = jnp.where(left, run_cols[0], run_cols[1])
            total = skip_ref[:, cols] * dy
            run_parts, direct_parts = [], [0.0, 0.0]
            for side in range(2):
                run_row = runt_ref[pl.ds(2 * p + side, 1), rows]
                step_row = stept_ref[pl.ds(2 * p + side, 1), rows]
                decay = jnp.exp(jnp.where(lower(GROUP), run_cols[side] - run_row, -jnp.inf))
                mine = left if side == 0 else ~left
                dy_mine = jnp.where(mine, dy, 0.0)
                near = low_dot(dy_mine, part, TAIL) * decay
                direct = near * pair_ref[block]
                both_ref[block] += near * step_row
                colt_ref[pl.ds(2 * p + side, 1), rows] = jnp.sum(direct, axis=0, keepdims=True)
                run_parts.append(jnp.sum(direct * step_row, axis=1, keepdims=True))
                total = total + low_dot(pair_ref[block] * decay * step_row, dy_mine, LEAD)
            if block == 1:
                grown = jnp.exp(run) * dy
                extra = split_sum(grown * low_dot(c_rows, kept, TAIL))
                bcg_ref[rows, state:] += low_dot(grown, kept, PLAIN)
                later = low_dot(grown, c_rows, LEAD)
                run_parts = [run_parts[side] + extra[side] for side in range(2)]
            else:
                step = jnp.where(
                    left, pick(step_ref[rows, :], 2 * p), pick(step_ref[rows, :], 2 * p + 1)
                )
                fall = jnp.exp(run[GROUP - 1 :] - run)
                to_end = fall * step
                back = low_dot(b_rows, later, TAIL)
                total = total + to_end * back
                direct_parts = split_sum(fall * part * back)
                extra = split_sum(to_end * part * back)
                bcg_ref[rows, :state] += low_dot(to_end * part, later, PLAIN)
                last = lax.broadcasted_iota(jnp.int32, (GROUP, 1), 0) == GROUP - 1
                run_parts = [
                    run_parts[side]
                    - extra[side]
                    + jnp.where(last, jnp.sum(extra[side], axis=0, keepdims=True), 0.0)
                    for side in range(2)
                ]
                direct_ref[rows, :] += jnp.where(
                    lane == 2 * p, direct_parts[0], 0.0
                ) + jnp.where(lane == 2 * p + 1, direct_parts[1], 0.0)
            run_grad_ref[rows, :] += jnp.where(lane == 2 * p, run_parts[0], 0.0) + jnp.where(
                lane == 2 * p + 1, run_parts[1], 0.0
            )
            pieces[block] = total
        du = jnp.concatenate(pieces, axis=0) * act * (1.0 + u * (1.0 - act))
        rows_ref[4:5, cols] = jnp.sum(du, axis=0, keepdims=True)
        back = 0.0
        for k in range(taps):
            rows_ref[k : k + 1, cols] = jnp.sum(
                du * shifted(pre, taps - 1 - k), axis=0, keepdims=True
            )
            back = back + cx_ref[k : k + 1, cols] * shifted(du, k - taps + 1)
        xlow_ref[:, cols] = back.astype(jnp.bfloat16)
        return carry

    lax.fori_loop(0, gate_ref.shape[1] // LANES, pair_step, 0)
    rate = -jnp.exp(alog_ref[...])
    upper = lower(GROUP).astype(jnp.float32)
    for block in range(2):
        rows = slice(block * GROUP, (block + 1) * GROUP)
        b_rows, c_rows = bc_low_ref[rows, :state], bc_low_ref[rows, state:]
        bcg_ref[rows, :state] += low_dot(both_ref[block], c_rows, LEAD)
        bcg_ref[rows, state:] += low_dot(both_ref[block], b_rows, PLAIN)
        direct = colt_ref[:, rows].T
        step = step_ref[rows, :]
        run_grad = run_grad_ref[rows, :] - direct * step
        suffix = lax.dot_general(
            upper, run_grad, (LEAD, ((), ())), precision=precise, preferred_element_type=jnp.float32
        )
        sig = jax.nn.sigmoid(dt_ref[rows, :] + dtb_ref[...])
        dt_grad = (direct_ref[rows, :] + direct + rate * suffix) * sig
        dtlow_ref[rows, :] = dt_grad.astype(jnp.bfloat16)
        heads_ref[0:1, :] += jnp.sum(dt_grad, axis=0, keepdims=True)
        heads_ref[1:2, :] += rate * jnp.sum(step * suffix, axis=0, keepdims=True)
    y_ref[...] = low_dot(gout_ref[...], wout_ref[...], PLAIN)
    partial_ref[...] = (
        low_dot(glow_ref[...], wz_ref[...], TAIL)
        + low_dot(xlow_ref[...], wx_ref[...], TAIL)
        + low_dot(dtlow_ref[...], wdt_ref[...], TAIL)
    )


def local_call(body, name, outs, scratch, *operands):
    vmem = pl.BlockSpec(memory_space=pltpu.VMEM)
    return pl.pallas_call(
        body,
        out_shape=tuple(jax.ShapeDtypeStruct(shape, kind) for shape, kind in outs),
        in_specs=[vmem] * len(operands),
        out_specs=(vmem,) * len(outs),
        scratch_shapes=scratch,
        compiler_params=pltpu.CompilerParams(vmem_limit_bytes=44 * 2**20),
        name=name,
    )(*operands)


PACK_ROWS = 16


def bit_orders(levels):
    if levels == 4:
        return ((0, 1, 2, 3), (1, 0, 2, 3), (2, 3, 0, 1))
    base = tuple(range(levels))
    third = max(1, levels // 3)
    return (base, base[third:] + base[:third], base[2 * third :] + base[: 2 * third])


def reduce_kernel(
    orders, a_ref, b_ref, c_ref, pack_ref, oa_ref, ob_ref, oc_ref, opack_ref,
    ra_ref, rb_ref, rc_ref, rpack_ref, spack_ref, send_sem, recv_sem, psend_sem, precv_sem,
):
    parts, outs, lands = (a_ref, b_ref, c_ref), (oa_ref, ob_ref, oc_ref), (ra_ref, rb_ref, rc_ref)
    levels = len(orders[0])
    count = 2**levels
    sizes = [count // 2 ** (stage + 1) for stage in range(levels)]
    starts = [sum(sizes[:stage]) for stage in range(levels)]
    me = lax.axis_index("dp")

    def my_bit(bit):
        return (me // 2**bit) % 2

    def partner(bit):
        return me + (1 - 2 * my_bit(bit)) * 2**bit

    def first_chunk(order, k, kept):
        own = my_bit(order[0])
        chunk = (own if kept else 1 - own) * 2 ** order[0]
        for place in range(1, levels):
            relative = (k // 2 ** (levels - 1 - place)) % 2
            chunk = chunk + ((my_bit(order[place]) + relative + 1) % 2) * 2 ** order[place]
        return chunk

    def transfer(g, stage, k):
        if stage == 0:
            source = parts[g].at[first_chunk(orders[g], k, False)]
        else:
            source = lands[g].at[starts[stage - 1] + k]
        slot = starts[stage] + k
        return pltpu.make_async_remote_copy(
            src_ref=source,
            dst_ref=lands[g].at[slot],
            send_sem=send_sem.at[g, slot],
            recv_sem=recv_sem.at[g, slot],
            device_id={"dp": partner(orders[g][stage])},
            device_id_type=pl.DeviceIdType.MESH,
        )

    def pack_transfer(stage):
        return pltpu.make_async_remote_copy(
            src_ref=pack_ref if stage == 0 else spack_ref.at[stage - 1],
            dst_ref=rpack_ref.at[stage],
            send_sem=psend_sem.at[stage],
            recv_sem=precv_sem.at[stage],
            device_id={"dp": partner(stage)},
            device_id_type=pl.DeviceIdType.MESH,
        )

    barrier = pltpu.get_barrier_semaphore()
    for bit in range(levels):
        pl.semaphore_signal(
            barrier, inc=1, device_id={"dp": partner(bit)}, device_id_type=pl.DeviceIdType.MESH
        )
    pl.semaphore_wait(barrier, levels)

    def begin(k, carry):
        for g in range(3):
            transfer(g, 0, k).start()
        return carry

    pack_transfer(0).start()
    lax.fori_loop(0, sizes[0], begin, 0)
    for stage in range(levels):
        half = sizes[stage] // 2
        for g in range(3):

            def step(k, carry, g=g, stage=stage, forward=False):
                transfer(g, stage, k).wait_recv()
                slot = starts[stage] + k
                if stage == 0:
                    own = parts[g][first_chunk(orders[g], k, True)]
                else:
                    own = lands[g][starts[stage - 1] + sizes[stage] + k]
                total = lands[g][slot] + own
                if stage == levels - 1:
                    outs[g][...] = total
                else:
                    lands[g][slot] = total
                if forward:
                    transfer(g, stage + 1, k).start()
                return carry

            if stage < levels - 1:
                lax.fori_loop(0, half, functools.partial(step, forward=True), 0)
                lax.fori_loop(half, sizes[stage], step, 0)
            else:
                step(0, 0)
        pack_transfer(stage).wait_recv()
        before = pack_ref[...] if stage == 0 else spack_ref[stage - 1]
        pack_total = before + rpack_ref[stage]
        if stage == levels - 1:
            opack_ref[...] = pack_total
        else:
            spack_ref[stage] = pack_total
            pack_transfer(stage + 1).start()
    for stage in range(levels):
        pack_transfer(stage).wait_send()

        def finish(k, carry, stage=stage):
            for g in range(3):
                transfer(g, stage, k).wait_send()
            return carry

        lax.fori_loop(0, sizes[stage], finish, 0)


def reduce_all(a, b, c, pack):
    count, rows, width = a.shape
    levels = count.bit_length() - 1
    vmem = pl.BlockSpec(memory_space=pltpu.VMEM)
    part = jax.ShapeDtypeStruct((rows, width), jnp.float32)
    return pl.pallas_call(
        functools.partial(reduce_kernel, bit_orders(levels)),
        out_shape=(part, part, part, jax.ShapeDtypeStruct(pack.shape, jnp.float32)),
        in_specs=[vmem] * 4,
        out_specs=(vmem,) * 4,
        scratch_shapes=[pltpu.VMEM((count - 1, rows, width), jnp.float32)] * 3
        + [
            pltpu.VMEM((levels,) + pack.shape, jnp.float32),
            pltpu.VMEM((levels,) + pack.shape, jnp.float32),
            pltpu.SemaphoreType.DMA((3, count - 1)),
            pltpu.SemaphoreType.DMA((3, count - 1)),
            pltpu.SemaphoreType.DMA((levels,)),
            pltpu.SemaphoreType.DMA((levels,)),
        ],
        compiler_params=pltpu.CompilerParams(
            collective_id=0, has_side_effects=True, vmem_limit_bytes=44 * 2**20
        ),
        name="reduce_all",
    )(a, b, c, pack)


def on_device(
    x_in,
    cotangent,
    norm_gain,
    w_z,
    w_x,
    w_bc,
    w_dt,
    conv_x,
    conv_x_bias,
    conv_bc,
    conv_bc_bias,
    dt_bias,
    a_log,
    d_skip,
    gate_norm,
    w_out,
):
    row_count, model_width = x_in.shape
    pair_count = lax.axis_size("tensor")
    half_width = model_width // pair_count
    col_start = lax.axis_index("tensor") * half_width
    inner_width = w_z.shape[1]
    heads_here = dt_bias.shape[0]
    total_width = inner_width * pair_count
    tokens = x_in.astype(jnp.float32)
    inv_rms = lax.rsqrt(jnp.mean(tokens * tokens, axis=1, keepdims=True) + epsilon)
    x_hat = tokens * inv_rms
    bc_width = w_bc.shape[1]

    def head_row(vector):
        return jnp.pad(vector, (0, LANES - heads_here))[None, :]

    w_dt_padded = jnp.pad(w_dt, ((0, 0), (0, LANES - heads_here)))
    skip_row = jnp.repeat(d_skip, inner_width // heads_here)[None, :]
    wide = (row_count, inner_width)
    shared = (
        conv_x,
        conv_x_bias[None, :],
        conv_bc,
        conv_bc_bias[None, :],
        head_row(dt_bias),
        head_row(a_log),
        skip_row,
        gate_norm[None, :],
        w_out,
    )
    normed, gate_pre, x_pre, bc_pre, dt_pre, mixed_out, out_grad, states, sums = local_call(
        forward_kernel,
        "forward",
        (
            ((row_count, model_width), jnp.bfloat16),
            (wide, jnp.float32),
            (wide, jnp.float32),
            ((row_count, bc_width), jnp.float32),
            ((row_count, LANES), jnp.float32),
            (wide, jnp.float32),
            (wide, jnp.float32),
            ((inner_width, bc_width // 2), jnp.float32),
            ((row_count, LANES), jnp.float32),
        ),
        prepare_scratch(row_count, bc_width),
        x_in, cotangent, norm_gain[None, :], w_z, w_x, w_bc, w_dt_padded, *shared,
    )
    sums = lax.psum(sums, "tensor")
    gate_out, y_part, gate_low, x_pre_low, dt_padded, bc_part_grad, partial_grad, rows, heads = (
        local_call(
            functools.partial(backward_kernel, total_width),
            "backward",
            (
                (wide, jnp.bfloat16),
                ((row_count, model_width), jnp.float32),
                (wide, jnp.bfloat16),
                (wide, jnp.bfloat16),
                ((row_count, LANES), jnp.bfloat16),
                ((row_count, bc_width), jnp.float32),
                ((row_count, model_width), jnp.float32),
                ((8, inner_width), jnp.float32),
                ((8, LANES), jnp.float32),
            ),
            prepare_scratch(row_count, bc_width)
            + [
                pltpu.VMEM((row_count, LANES), jnp.float32),
                pltpu.VMEM((row_count, LANES), jnp.float32),
                pltpu.VMEM((LANES, row_count), jnp.float32),
                pltpu.VMEM((2, GROUP, GROUP), jnp.float32),
            ],
            sums, gate_pre, x_pre, bc_pre, dt_pre, mixed_out, out_grad, states,
            w_z, w_x, w_dt_padded, *shared,
        )
    )
    out_share = lax.psum_scatter(y_part, "tensor", scatter_dimension=1, tiled=True)
    token_half = lax.dynamic_slice_in_dim(tokens, col_start, half_width, 1)
    result = (token_half + out_share).astype(jnp.bfloat16)
    w_out_grad = lead_contract(cotangent, gate_out)
    bc_conv_grad = lax.psum(bc_part_grad, "tensor")
    bc_conv_back = jax.vjp(
        lambda *pieces: jax.nn.silu(causal_conv(*pieces)), bc_pre, conv_bc, conv_bc_bias
    )[1]
    bc_pre_grad, conv_bc_grad, conv_bc_bias_grad = bc_conv_back(bc_conv_grad)
    bc_pre_low = bc_pre_grad.astype(jnp.bfloat16)
    conv_taps = conv_x.shape[0]
    hat_half = lax.dynamic_slice_in_dim(x_hat, col_start, half_width, 1)
    gain_half = lax.dynamic_slice_in_dim(norm_gain, col_start, half_width, 0)
    normed_grad = lax.psum(partial_grad, "tensor") + tail_contract(bc_pre_low, w_bc)
    grad_half = lax.dynamic_slice_in_dim(normed_grad, col_start, half_width, 1)
    weighted_in = grad_half * gain_half[None, :]
    in_dot = jnp.sum(normed_grad * norm_gain[None, :] * x_hat, axis=1)
    norm_gain_grad = jnp.sum(grad_half * hat_half, axis=0)
    cot_half = lax.dynamic_slice_in_dim(cotangent, col_start, half_width, 1).astype(jnp.float32)
    x_grad = (cot_half + inv_rms * (weighted_in - hat_half * in_dot[:, None] / model_width)).astype(
        jnp.bfloat16
    )
    count = lax.axis_size("dp")
    half_bc = bc_pre_low.shape[1] // 2

    def chunks(array):
        return array.reshape(count, model_width // count, array.shape[1])

    part_a = chunks(jnp.concatenate([w_out_grad, lead_contract(normed, dt_padded)], axis=1))
    part_b = chunks(
        lead_contract(normed, jnp.concatenate([gate_low, bc_pre_low[:, :half_bc]], axis=1))
    )
    part_c = chunks(
        lead_contract(normed, jnp.concatenate([x_pre_low, bc_pre_low[:, half_bc:]], axis=1))
    )
    small = (
        rows,
        conv_bc_grad,
        conv_bc_bias_grad,
        heads[:2],
        norm_gain_grad,
    )
    flat = jnp.concatenate([array.reshape(-1) for array in small])
    pack = jnp.pad(flat, (0, PACK_ROWS * 768 - flat.shape[0])).reshape(PACK_ROWS, 768)
    sum_a, sum_b, sum_c, pack_total = reduce_all(part_a, part_b, part_c, pack)
    w_out_share = jnp.transpose(sum_a[:, :inner_width])
    w_dt_share = sum_a[:, inner_width : inner_width + heads_here]
    w_z_share = sum_b[:, :inner_width]
    w_x_share = sum_c[:, :inner_width]
    w_bc_share = jnp.concatenate([sum_b[:, inner_width:], sum_c[:, inner_width:]], axis=1)
    flat_total = pack_total.reshape(-1)
    totals, at = [], 0
    for array in small:
        totals.append(flat_total[at : at + array.size].reshape(array.shape))
        at += array.size
    rows_total, conv_bc_total, conv_bc_bias_total, heads_total, norm_gain_total = totals
    conv_x_total = rows_total[:conv_taps]
    conv_x_bias_total = rows_total[conv_taps]
    gate_norm_total = rows_total[conv_taps + 1]
    d_skip_total = jnp.sum(rows_total[conv_taps + 2].reshape(heads_here, -1), axis=1)
    dt_bias_total = heads_total[0, :heads_here]
    a_log_total = heads_total[1, :heads_here]
    return (
        result,
        x_grad,
        norm_gain_total,
        w_z_share,
        w_x_share,
        w_bc_share,
        w_dt_share,
        conv_x_total,
        conv_x_bias_total,
        conv_bc_total,
        conv_bc_bias_total,
        dt_bias_total,
        a_log_total,
        d_skip_total,
        gate_norm_total,
        w_out_share,
    )


def solution(mesh):
    in_specs = (
        P("dp", None),
        P("dp", None),
        P(),
        P(None, "tensor"),
        P(None, "tensor"),
        P(),
        P(None, "tensor"),
        P(None, "tensor"),
        P("tensor"),
        P(),
        P(),
        P("tensor"),
        P("tensor"),
        P("tensor"),
        P("tensor"),
        P("tensor", None),
    )
    out_specs = (
        P("dp", "tensor"),
        P("dp", "tensor"),
        P("tensor"),
        P("dp", "tensor"),
        P("dp", "tensor"),
        P("dp", None),
        P("dp", "tensor"),
        P(None, "tensor"),
        P("tensor"),
        P(),
        P(),
        P("tensor"),
        P("tensor"),
        P("tensor"),
        P("tensor"),
        P("tensor", "dp"),
    )
    return jax.shard_map(
        on_device, mesh=mesh, in_specs=in_specs, out_specs=out_specs, check_vma=False
    )
```

```python
import functools

import jax
import jax.numpy as jnp
from jax import lax
from jax.experimental import pallas as pl
from jax.experimental.pallas import tpu as pltpu
from jax.sharding import PartitionSpec as P

GROUP = 256


epsilon = 1e-05
precise = lax.Precision.HIGHEST


def lead_contract(left, right):
    return lax.dot_general(
        left, right, (((0,), (0,)), ((), ())), preferred_element_type=jnp.float32
    )


def tail_contract(left, right):
    return lax.dot_general(
        left, right, (((1,), (1,)), ((), ())), preferred_element_type=jnp.float32
    )


def causal_conv(pre_conv, kernel, offset):
    taps = kernel.shape[0]
    padded = jnp.pad(pre_conv, ((taps - 1, 0), (0, 0)))
    summed = offset[None, :] + kernel[0][None, :] * padded[: pre_conv.shape[0]]
    for tap_index in range(1, taps):
        summed = (
            summed + kernel[tap_index][None, :] * padded[tap_index : tap_index + pre_conv.shape[0]]
        )
    return summed


LANES = 128


def low_dot(left, right, contract):
    return lax.dot_general(
        left.astype(jnp.bfloat16),
        right.astype(jnp.bfloat16),
        ((contract[0], contract[1]), ((), ())),
        preferred_element_type=jnp.float32,
    )


PLAIN, LEAD, TAIL = ((1,), (0,)), ((0,), (0,)), ((1,), (1,))


def shifted(rows, distance):
    if distance == 0:
        return rows
    length = rows.shape[0]
    at = lax.broadcasted_iota(jnp.int32, rows.shape, 0)
    moved = pltpu.roll(rows, distance % length, 0)
    keep = at >= distance if distance > 0 else at < length + distance
    return jnp.where(keep, moved, 0.0)


def conv_rows(pre, taps, offset):
    count = taps.shape[0]
    total = offset + taps[count - 1 : count] * pre
    for k in range(count - 1):
        total = total + taps[k : k + 1] * shifted(pre, count - 1 - k)
    return total


def pick(array, head):
    lane = lax.broadcasted_iota(jnp.int32, array.shape, 1)
    return jnp.sum(jnp.where(lane == head, array, 0.0), axis=1, keepdims=True)


def lower(size):
    return lax.broadcasted_iota(jnp.int32, (size, size), 0) >= lax.broadcasted_iota(
        jnp.int32, (size, size), 1
    )


def prepare(dt_ref, dtb_ref, alog_ref, bc_ref, cbc_ref, cbcb_ref, scratch):
    step_ref, run_ref, stept_ref, runt_ref, bc_low_ref, pair_ref = scratch
    step = dt_ref[...] + dtb_ref[...]
    step = jnp.maximum(step, 0.0) + jnp.log1p(jnp.exp(-jnp.abs(step)))
    step_ref[...] = step
    decay = step * -jnp.exp(alog_ref[...])
    u = conv_rows(bc_ref[...], cbc_ref[...], cbcb_ref[...])
    bc_low_ref[...] = (u * jax.nn.sigmoid(u)).astype(jnp.bfloat16)
    state = bc_low_ref.shape[1] // 2
    tri = lower(GROUP).astype(jnp.float32)
    for block in range(2):
        rows = slice(block * GROUP, (block + 1) * GROUP)
        run = jnp.dot(tri, decay[rows], precision=precise, preferred_element_type=jnp.float32)
        run_ref[rows, :] = run
        runt_ref[:, rows] = run.T
        stept_ref[:, rows] = step[rows].T
        pair_ref[block] = low_dot(bc_low_ref[rows, state:], bc_low_ref[rows, :state], TAIL)


def prepare_scratch(rows, width):
    return [
        pltpu.VMEM((rows, LANES), jnp.float32),
        pltpu.VMEM((rows, LANES), jnp.float32),
        pltpu.VMEM((LANES, rows), jnp.float32),
        pltpu.VMEM((LANES, rows), jnp.float32),
        pltpu.VMEM((rows, width), jnp.bfloat16),
        pltpu.VMEM((2, GROUP, GROUP), jnp.float32),
    ]


def forward_kernel(
    x_ref, cot_ref, gain_ref, wz_ref, wx_ref, wbc_ref, wdt_ref, cx_ref, cxb_ref, cbc_ref, cbcb_ref,
    dtb_ref, alog_ref, skip_ref, gnorm_ref, wout_ref,
    normed_ref, gate_ref, xpre_ref, bc_ref, dt_ref, mixed_ref, og_ref, state_ref, sums_ref,
    *scratch,
):
    step_ref, run_ref, stept_ref, runt_ref, bc_low_ref, pair_ref = scratch
    tokens = x_ref[...].astype(jnp.float32)
    inv_rms = lax.rsqrt(jnp.mean(tokens * tokens, axis=1, keepdims=True) + epsilon)
    normed_ref[...] = (tokens * inv_rms * gain_ref[...]).astype(jnp.bfloat16)
    bc_ref[...] = low_dot(normed_ref[...], wbc_ref[...], PLAIN)
    dt_ref[...] = low_dot(normed_ref[...], wdt_ref[...], PLAIN)
    prepare(dt_ref, dtb_ref, alog_ref, bc_ref, cbc_ref, cbcb_ref, scratch)
    sums_ref[...] = jnp.zeros_like(sums_ref)
    state = bc_low_ref.shape[1] // 2
    lane = lax.broadcasted_iota(jnp.int32, (1, LANES), 1)
    left = lane < LANES // 2

    def pair_step(p, carry):
        cols = pl.ds(pl.multiple_of(p * LANES, LANES), LANES)
        pre = low_dot(normed_ref[...], wx_ref[:, cols], PLAIN)
        xpre_ref[:, cols] = pre
        gate = low_dot(normed_ref[...], wz_ref[:, cols], PLAIN)
        gate_ref[:, cols] = gate
        u = conv_rows(pre, cx_ref[:, cols], cxb_ref[:, cols])
        x_low = (u * jax.nn.sigmoid(u)).astype(jnp.bfloat16)
        values = x_low.astype(jnp.float32)
        carried_state = None
        for block in range(2):
            rows = slice(block * GROUP, (block + 1) * GROUP)
            part = values[rows]
            b_rows, c_rows = bc_low_ref[rows, :state], bc_low_ref[rows, state:]
            run_cols = [pick(run_ref[rows, :], 2 * p + side) for side in range(2)]
            total = skip_ref[:, cols] * part
            for side in range(2):
                run_row = runt_ref[pl.ds(2 * p + side, 1), rows]
                step_row = stept_ref[pl.ds(2 * p + side, 1), rows]
                differ = jnp.where(lower(GROUP), run_cols[side] - run_row, -jnp.inf)
                weights = pair_ref[block] * jnp.exp(differ) * step_row
                mine = left if side == 0 else ~left
                total = total + low_dot(weights, jnp.where(mine, part, 0.0), PLAIN)
            run = jnp.where(left, run_cols[0], run_cols[1])
            if block == 0:
                step = jnp.where(
                    left, pick(step_ref[rows, :], 2 * p), pick(step_ref[rows, :], 2 * p + 1)
                )
                to_end = jnp.exp(run[GROUP - 1 :] - run) * step
                carried_state = low_dot(to_end * part, b_rows, LEAD)
                state_ref[cols, :] = carried_state
            else:
                total = total + jnp.exp(run) * low_dot(c_rows, carried_state, TAIL)
            mixed_ref[rows, cols] = total
        gated = mixed_ref[:, cols] * gate * jax.nn.sigmoid(gate)
        og = low_dot(cot_ref[...], wout_ref[cols, :], TAIL)
        og_ref[:, cols] = og
        square = jnp.sum(gated * gated, axis=1, keepdims=True)
        inner = jnp.sum(og * gnorm_ref[:, cols] * gated, axis=1, keepdims=True)
        sums_ref[...] += jnp.where(lane == 0, square, 0.0) + jnp.where(lane == 1, inner, 0.0)
        return carry

    lax.fori_loop(0, gate_ref.shape[1] // LANES, pair_step, 0)


def backward_kernel(
    total_width,
    sums_ref, gate_ref, xpre_ref, bc_ref, dt_ref, mixed_ref, og_ref, state_ref,
    wz_ref, wx_ref, wdt_ref, cx_ref, cxb_ref, cbc_ref, cbcb_ref, dtb_ref, alog_ref, skip_ref,
    gnorm_ref, wout_ref,
    gout_ref, y_ref, glow_ref, xlow_ref, dtlow_ref, bcg_ref, partial_ref, rows_ref, heads_ref,
    *scratch,
):
    step_ref, run_ref, stept_ref, runt_ref, bc_low_ref, pair_ref = scratch[:6]
    run_grad_ref, direct_ref, colt_ref, both_ref = scratch[6:]
    prepare(dt_ref, dtb_ref, alog_ref, bc_ref, cbc_ref, cbcb_ref, scratch[:6])
    for ref in (run_grad_ref, direct_ref, colt_ref, both_ref, bcg_ref, rows_ref, heads_ref):
        ref[...] = jnp.zeros_like(ref)
    state = bc_low_ref.shape[1] // 2
    lane = lax.broadcasted_iota(jnp.int32, (1, LANES), 1)
    left = lane < LANES // 2
    taps = cx_ref.shape[0]

    def split_sum(array):
        return (
            jnp.sum(jnp.where(left, array, 0.0), axis=1, keepdims=True),
            jnp.sum(jnp.where(left, 0.0, array), axis=1, keepdims=True),
        )

    def pair_step(p, carry):
        cols = pl.ds(pl.multiple_of(p * LANES, LANES), LANES)
        spread = lax.rsqrt(sums_ref[:, 0:1] / total_width + epsilon)
        row_dot = sums_ref[:, 1:2]
        gate, mixed, og = gate_ref[:, cols], mixed_ref[:, cols], og_ref[:, cols]
        sigma = jax.nn.sigmoid(gate)
        gate_act = gate * sigma
        gated = mixed * gate_act
        gout_ref[:, cols] = (gated * spread * gnorm_ref[:, cols]).astype(jnp.bfloat16)
        rows_ref[5:6, cols] = jnp.sum(og * gated * spread, axis=0, keepdims=True)
        gated_grad = spread * og * gnorm_ref[:, cols] - gated * (
            spread * spread * spread * row_dot / total_width
        )
        grad = gated_grad * gate_act
        glow_ref[:, cols] = (
            gated_grad * mixed * sigma * (1.0 + gate * (1.0 - sigma))
        ).astype(jnp.bfloat16)
        pre = xpre_ref[:, cols]
        u = conv_rows(pre, cx_ref[:, cols], cxb_ref[:, cols])
        act = jax.nn.sigmoid(u)
        values = (u * act).astype(jnp.bfloat16).astype(jnp.float32)
        rows_ref[6:7, cols] = jnp.sum(grad * values, axis=0, keepdims=True)
        kept = state_ref[cols, :]
        later = None
        pieces = [None, None]
        for block in (1, 0):
            rows = slice(block * GROUP, (block + 1) * GROUP)
            part, dy = values[rows], grad[rows]
            b_rows, c_rows = bc_low_ref[rows, :state], bc_low_ref[rows, state:]
            run_cols = [pick(run_ref[rows, :], 2 * p + side) for side in range(2)]
            run = jnp.where(left, run_cols[0], run_cols[1])
            total = skip_ref[:, cols] * dy
            run_parts, direct_parts = [], [0.0, 0.0]
            for side in range(2):
                run_row = runt_ref[pl.ds(2 * p + side, 1), rows]
                step_row = stept_ref[pl.ds(2 * p + side, 1), rows]
                decay = jnp.exp(jnp.where(lower(GROUP), run_cols[side] - run_row, -jnp.inf))
                mine = left if side == 0 else ~left
                dy_mine = jnp.where(mine, dy, 0.0)
                near = low_dot(dy_mine, part, TAIL) * decay
                direct = near * pair_ref[block]
                both_ref[block] += near * step_row
                colt_ref[pl.ds(2 * p + side, 1), rows] = jnp.sum(direct, axis=0, keepdims=True)
                run_parts.append(jnp.sum(direct * step_row, axis=1, keepdims=True))
                total = total + low_dot(pair_ref[block] * decay * step_row, dy_mine, LEAD)
            if block == 1:
                grown = jnp.exp(run) * dy
                extra = split_sum(grown * low_dot(c_rows, kept, TAIL))
                bcg_ref[rows, state:] += low_dot(grown, kept, PLAIN)
                later = low_dot(grown, c_rows, LEAD)
                run_parts = [run_parts[side] + extra[side] for side in range(2)]
            else:
                step = jnp.where(
                    left, pick(step_ref[rows, :], 2 * p), pick(step_ref[rows, :], 2 * p + 1)
                )
                fall = jnp.exp(run[GROUP - 1 :] - run)
                to_end = fall * step
                back = low_dot(b_rows, later, TAIL)
                total = total + to_end * back
                direct_parts = split_sum(fall * part * back)
                extra = split_sum(to_end * part * back)
                bcg_ref[rows, :state] += low_dot(to_end * part, later, PLAIN)
                last = lax.broadcasted_iota(jnp.int32, (GROUP, 1), 0) == GROUP - 1
                run_parts = [
                    run_parts[side]
                    - extra[side]
                    + jnp.where(last, jnp.sum(extra[side], axis=0, keepdims=True), 0.0)
                    for side in range(2)
                ]
                direct_ref[rows, :] += jnp.where(
                    lane == 2 * p, direct_parts[0], 0.0
                ) + jnp.where(lane == 2 * p + 1, direct_parts[1], 0.0)
            run_grad_ref[rows, :] += jnp.where(lane == 2 * p, run_parts[0], 0.0) + jnp.where(
                lane == 2 * p + 1, run_parts[1], 0.0
            )
            pieces[block] = total
        du = jnp.concatenate(pieces, axis=0) * act * (1.0 + u * (1.0 - act))
        rows_ref[4:5, cols] = jnp.sum(du, axis=0, keepdims=True)
        back = 0.0
        for k in range(taps):
            rows_ref[k : k + 1, cols] = jnp.sum(
                du * shifted(pre, taps - 1 - k), axis=0, keepdims=True
            )
            back = back + cx_ref[k : k + 1, cols] * shifted(du, k - taps + 1)
        xlow_ref[:, cols] = back.astype(jnp.bfloat16)
        return carry

    lax.fori_loop(0, gate_ref.shape[1] // LANES, pair_step, 0)
    rate = -jnp.exp(alog_ref[...])
    upper = lower(GROUP).astype(jnp.float32)
    for block in range(2):
        rows = slice(block * GROUP, (block + 1) * GROUP)
        b_rows, c_rows = bc_low_ref[rows, :state], bc_low_ref[rows, state:]
        bcg_ref[rows, :state] += low_dot(both_ref[block], c_rows, LEAD)
        bcg_ref[rows, state:] += low_dot(both_ref[block], b_rows, PLAIN)
        direct = colt_ref[:, rows].T
        step = step_ref[rows, :]
        run_grad = run_grad_ref[rows, :] - direct * step
        suffix = lax.dot_general(
            upper, run_grad, (LEAD, ((), ())), precision=precise, preferred_element_type=jnp.float32
        )
        sig = jax.nn.sigmoid(dt_ref[rows, :] + dtb_ref[...])
        dt_grad = (direct_ref[rows, :] + direct + rate * suffix) * sig
        dtlow_ref[rows, :] = dt_grad.astype(jnp.bfloat16)
        heads_ref[0:1, :] += jnp.sum(dt_grad, axis=0, keepdims=True)
        heads_ref[1:2, :] += rate * jnp.sum(step * suffix, axis=0, keepdims=True)
    y_ref[...] = low_dot(gout_ref[...], wout_ref[...], PLAIN)
    partial_ref[...] = (
        low_dot(glow_ref[...], wz_ref[...], TAIL)
        + low_dot(xlow_ref[...], wx_ref[...], TAIL)
        + low_dot(dtlow_ref[...], wdt_ref[...], TAIL)
    )


def local_call(body, name, outs, scratch, *operands):
    vmem = pl.BlockSpec(memory_space=pltpu.VMEM)
    return pl.pallas_call(
        body,
        out_shape=tuple(jax.ShapeDtypeStruct(shape, kind) for shape, kind in outs),
        in_specs=[vmem] * len(operands),
        out_specs=(vmem,) * len(outs),
        scratch_shapes=scratch,
        compiler_params=pltpu.CompilerParams(vmem_limit_bytes=44 * 2**20),
        name=name,
    )(*operands)


PACK_ROWS = 16


def bit_orders(levels):
    if levels == 4:
        return ((0, 1, 2, 3), (1, 0, 2, 3), (2, 3, 0, 1))
    base = tuple(range(levels))
    third = max(1, levels // 3)
    return (base, base[third:] + base[:third], base[2 * third :] + base[: 2 * third])


def reduce_kernel(
    orders, a_ref, b_ref, c_ref, pack_ref, oa_ref, ob_ref, oc_ref, opack_ref,
    ra_ref, rb_ref, rc_ref, rpack_ref, spack_ref, send_sem, recv_sem, psend_sem, precv_sem,
):
    parts, outs, lands = (a_ref, b_ref, c_ref), (oa_ref, ob_ref, oc_ref), (ra_ref, rb_ref, rc_ref)
    levels = len(orders[0])
    count = 2**levels
    sizes = [count // 2 ** (stage + 1) for stage in range(levels)]
    starts = [sum(sizes[:stage]) for stage in range(levels)]
    me = lax.axis_index("dp")

    def my_bit(bit):
        return (me // 2**bit) % 2

    def partner(bit):
        return me + (1 - 2 * my_bit(bit)) * 2**bit

    def first_chunk(order, k, kept):
        own = my_bit(order[0])
        chunk = (own if kept else 1 - own) * 2 ** order[0]
        for place in range(1, levels):
            relative = (k // 2 ** (levels - 1 - place)) % 2
            chunk = chunk + ((my_bit(order[place]) + relative + 1) % 2) * 2 ** order[place]
        return chunk

    def transfer(g, stage, k):
        if stage == 0:
            source = parts[g].at[first_chunk(orders[g], k, False)]
        else:
            source = lands[g].at[starts[stage - 1] + k]
        slot = starts[stage] + k
        return pltpu.make_async_remote_copy(
            src_ref=source,
            dst_ref=lands[g].at[slot],
            send_sem=send_sem.at[g, slot],
            recv_sem=recv_sem.at[g, slot],
            device_id={"dp": partner(orders[g][stage])},
            device_id_type=pl.DeviceIdType.MESH,
        )

    def pack_transfer(stage):
        return pltpu.make_async_remote_copy(
            src_ref=pack_ref if stage == 0 else spack_ref.at[stage - 1],
            dst_ref=rpack_ref.at[stage],
            send_sem=psend_sem.at[stage],
            recv_sem=precv_sem.at[stage],
            device_id={"dp": partner(stage)},
            device_id_type=pl.DeviceIdType.MESH,
        )

    barrier = pltpu.get_barrier_semaphore()
    for bit in range(levels):
        pl.semaphore_signal(
            barrier, inc=1, device_id={"dp": partner(bit)}, device_id_type=pl.DeviceIdType.MESH
        )
    pl.semaphore_wait(barrier, levels)

    def begin(k, carry):
        for g in range(3):
            transfer(g, 0, k).start()
        return carry

    pack_transfer(0).start()
    lax.fori_loop(0, sizes[0], begin, 0)
    for stage in range(levels):
        half = sizes[stage] // 2
        for g in range(3):

            def step(k, carry, g=g, stage=stage, forward=False):
                transfer(g, stage, k).wait_recv()
                slot = starts[stage] + k
                if stage == 0:
                    own = parts[g][first_chunk(orders[g], k, True)]
                else:
                    own = lands[g][starts[stage - 1] + sizes[stage] + k]
                total = lands[g][slot] + own
                if stage == levels - 1:
                    outs[g][...] = total
                else:
                    lands[g][slot] = total
                if forward:
                    transfer(g, stage + 1, k).start()
                return carry

            if stage < levels - 1:
                lax.fori_loop(0, half, functools.partial(step, forward=True), 0)
                lax.fori_loop(half, sizes[stage], step, 0)
            else:
                step(0, 0)
        pack_transfer(stage).wait_recv()
        before = pack_ref[...] if stage == 0 else spack_ref[stage - 1]
        pack_total = before + rpack_ref[stage]
        if stage == levels - 1:
            opack_ref[...] = pack_total
        else:
            spack_ref[stage] = pack_total
            pack_transfer(stage + 1).start()
    for stage in range(levels):
        pack_transfer(stage).wait_send()

        def finish(k, carry, stage=stage):
            for g in range(3):
                transfer(g, stage, k).wait_send()
            return carry

        lax.fori_loop(0, sizes[stage], finish, 0)


def reduce_all(a, b, c, pack):
    count, rows, width = a.shape
    levels = count.bit_length() - 1
    vmem = pl.BlockSpec(memory_space=pltpu.VMEM)
    part = jax.ShapeDtypeStruct((rows, width), jnp.float32)
    return pl.pallas_call(
        functools.partial(reduce_kernel, bit_orders(levels)),
        out_shape=(part, part, part, jax.ShapeDtypeStruct(pack.shape, jnp.float32)),
        in_specs=[vmem] * 4,
        out_specs=(vmem,) * 4,
        scratch_shapes=[pltpu.VMEM((count - 1, rows, width), jnp.float32)] * 3
        + [
            pltpu.VMEM((levels,) + pack.shape, jnp.float32),
            pltpu.VMEM((levels,) + pack.shape, jnp.float32),
            pltpu.SemaphoreType.DMA((3, count - 1)),
            pltpu.SemaphoreType.DMA((3, count - 1)),
            pltpu.SemaphoreType.DMA((levels,)),
            pltpu.SemaphoreType.DMA((levels,)),
        ],
        compiler_params=pltpu.CompilerParams(
            collective_id=0, has_side_effects=True, vmem_limit_bytes=44 * 2**20
        ),
        name="reduce_all",
    )(a, b, c, pack)


def pair_kernel(halved, *refs):
    count = len(halved)
    sources, outs, lands = refs[:count], refs[count : 2 * count], refs[2 * count : 3 * count]
    send_sem, recv_sem = refs[3 * count :]
    me = lax.axis_index("tensor")
    other = 1 - me

    def view(i, owner):
        if not halved[i]:
            return sources[i]
        width = outs[i].shape[1]
        return sources[i].at[:, pl.ds(pl.multiple_of(owner * width, LANES), width)]

    barrier = pltpu.get_barrier_semaphore()
    pl.semaphore_signal(
        barrier, inc=1, device_id={"tensor": other}, device_id_type=pl.DeviceIdType.MESH
    )
    pl.semaphore_wait(barrier, 1)
    copies = [
        pltpu.make_async_remote_copy(
            src_ref=view(i, other),
            dst_ref=lands[i],
            send_sem=send_sem.at[i],
            recv_sem=recv_sem.at[i],
            device_id={"tensor": other},
            device_id_type=pl.DeviceIdType.MESH,
        )
        for i in range(count)
    ]
    for copy in copies:
        copy.start()
    for i in range(count):
        copies[i].wait_recv()
        outs[i][...] = view(i, me)[...] + lands[i][...]
    for copy in copies:
        copy.wait_send()


def pair_sum(arrays, halved, number):
    vmem = pl.BlockSpec(memory_space=pltpu.VMEM)
    shapes = [
        (array.shape[0], array.shape[1] // 2 if half else array.shape[1])
        for array, half in zip(arrays, halved)
    ]
    return pl.pallas_call(
        functools.partial(pair_kernel, halved),
        out_shape=tuple(jax.ShapeDtypeStruct(shape, jnp.float32) for shape in shapes),
        in_specs=[vmem] * len(arrays),
        out_specs=(vmem,) * len(arrays),
        scratch_shapes=[pltpu.VMEM(shape, jnp.float32) for shape in shapes]
        + [pltpu.SemaphoreType.DMA((len(arrays),))] * 2,
        compiler_params=pltpu.CompilerParams(
            collective_id=number, has_side_effects=True, vmem_limit_bytes=24 * 2**20
        ),
        name="pair_sum",
    )(*arrays)


def on_device(
    x_in,
    cotangent,
    norm_gain,
    w_z,
    w_x,
    w_bc,
    w_dt,
    conv_x,
    conv_x_bias,
    conv_bc,
    conv_bc_bias,
    dt_bias,
    a_log,
    d_skip,
    gate_norm,
    w_out,
):
    row_count, model_width = x_in.shape
    pair_count = lax.axis_size("tensor")
    half_width = model_width // pair_count
    col_start = lax.axis_index("tensor") * half_width
    inner_width = w_z.shape[1]
    heads_here = dt_bias.shape[0]
    total_width = inner_width * pair_count
    tokens = x_in.astype(jnp.float32)
    inv_rms = lax.rsqrt(jnp.mean(tokens * tokens, axis=1, keepdims=True) + epsilon)
    x_hat = tokens * inv_rms
    bc_width = w_bc.shape[1]

    def head_row(vector):
        return jnp.pad(vector, (0, LANES - heads_here))[None, :]

    w_dt_padded = jnp.pad(w_dt, ((0, 0), (0, LANES - heads_here)))
    skip_row = jnp.repeat(d_skip, inner_width // heads_here)[None, :]
    wide = (row_count, inner_width)
    shared = (
        conv_x,
        conv_x_bias[None, :],
        conv_bc,
        conv_bc_bias[None, :],
        head_row(dt_bias),
        head_row(a_log),
        skip_row,
        gate_norm[None, :],
        w_out,
    )
    normed, gate_pre, x_pre, bc_pre, dt_pre, mixed_out, out_grad, states, sums = local_call(
        forward_kernel,
        "forward",
        (
            ((row_count, model_width), jnp.bfloat16),
            (wide, jnp.float32),
            (wide, jnp.float32),
            ((row_count, bc_width), jnp.float32),
            ((row_count, LANES), jnp.float32),
            (wide, jnp.float32),
            (wide, jnp.float32),
            ((inner_width, bc_width // 2), jnp.float32),
            ((row_count, LANES), jnp.float32),
        ),
        prepare_scratch(row_count, bc_width),
        x_in, cotangent, norm_gain[None, :], w_z, w_x, w_bc, w_dt_padded, *shared,
    )
    (sums,) = pair_sum((sums,), (False,), 1)
    gate_out, y_part, gate_low, x_pre_low, dt_padded, bc_part_grad, partial_grad, rows, heads = (
        local_call(
            functools.partial(backward_kernel, total_width),
            "backward",
            (
                (wide, jnp.bfloat16),
                ((row_count, model_width), jnp.float32),
                (wide, jnp.bfloat16),
                (wide, jnp.bfloat16),
                ((row_count, LANES), jnp.bfloat16),
                ((row_count, bc_width), jnp.float32),
                ((row_count, model_width), jnp.float32),
                ((8, inner_width), jnp.float32),
                ((8, LANES), jnp.float32),
            ),
            prepare_scratch(row_count, bc_width)
            + [
                pltpu.VMEM((row_count, LANES), jnp.float32),
                pltpu.VMEM((row_count, LANES), jnp.float32),
                pltpu.VMEM((LANES, row_count), jnp.float32),
                pltpu.VMEM((2, GROUP, GROUP), jnp.float32),
            ],
            sums, gate_pre, x_pre, bc_pre, dt_pre, mixed_out, out_grad, states,
            w_z, w_x, w_dt_padded, *shared,
        )
    )
    bc_conv_grad, partial_total, out_share = pair_sum(
        (bc_part_grad, partial_grad, y_part), (False, False, True), 2
    )
    token_half = lax.dynamic_slice_in_dim(tokens, col_start, half_width, 1)
    result = (token_half + out_share).astype(jnp.bfloat16)
    w_out_grad = lead_contract(cotangent, gate_out)
    bc_conv_back = jax.vjp(
        lambda *pieces: jax.nn.silu(causal_conv(*pieces)), bc_pre, conv_bc, conv_bc_bias
    )[1]
    bc_pre_grad, conv_bc_grad, conv_bc_bias_grad = bc_conv_back(bc_conv_grad)
    bc_pre_low = bc_pre_grad.astype(jnp.bfloat16)
    conv_taps = conv_x.shape[0]
    hat_half = lax.dynamic_slice_in_dim(x_hat, col_start, half_width, 1)
    gain_half = lax.dynamic_slice_in_dim(norm_gain, col_start, half_width, 0)
    normed_grad = partial_total + tail_contract(bc_pre_low, w_bc)
    grad_half = lax.dynamic_slice_in_dim(normed_grad, col_start, half_width, 1)
    weighted_in = grad_half * gain_half[None, :]
    in_dot = jnp.sum(normed_grad * norm_gain[None, :] * x_hat, axis=1)
    norm_gain_grad = jnp.sum(grad_half * hat_half, axis=0)
    cot_half = lax.dynamic_slice_in_dim(cotangent, col_start, half_width, 1).astype(jnp.float32)
    x_grad = (cot_half + inv_rms * (weighted_in - hat_half * in_dot[:, None] / model_width)).astype(
        jnp.bfloat16
    )
    count = lax.axis_size("dp")
    half_bc = bc_pre_low.shape[1] // 2

    def chunks(array):
        return array.reshape(count, model_width // count, array.shape[1])

    part_a = chunks(jnp.concatenate([w_out_grad, lead_contract(normed, dt_padded)], axis=1))
    part_b = chunks(
        lead_contract(normed, jnp.concatenate([gate_low, bc_pre_low[:, :half_bc]], axis=1))
    )
    part_c = chunks(
        lead_contract(normed, jnp.concatenate([x_pre_low, bc_pre_low[:, half_bc:]], axis=1))
    )
    small = (
        rows,
        conv_bc_grad,
        conv_bc_bias_grad,
        heads[:2],
        norm_gain_grad,
    )
    flat = jnp.concatenate([array.reshape(-1) for array in small])
    pack = jnp.pad(flat, (0, PACK_ROWS * 768 - flat.shape[0])).reshape(PACK_ROWS, 768)
    sum_a, sum_b, sum_c, pack_total = reduce_all(part_a, part_b, part_c, pack)
    w_out_share = jnp.transpose(sum_a[:, :inner_width])
    w_dt_share = sum_a[:, inner_width : inner_width + heads_here]
    w_z_share = sum_b[:, :inner_width]
    w_x_share = sum_c[:, :inner_width]
    w_bc_share = jnp.concatenate([sum_b[:, inner_width:], sum_c[:, inner_width:]], axis=1)
    flat_total = pack_total.reshape(-1)
    totals, at = [], 0
    for array in small:
        totals.append(flat_total[at : at + array.size].reshape(array.shape))
        at += array.size
    rows_total, conv_bc_total, conv_bc_bias_total, heads_total, norm_gain_total = totals
    conv_x_total = rows_total[:conv_taps]
    conv_x_bias_total = rows_total[conv_taps]
    gate_norm_total = rows_total[conv_taps + 1]
    d_skip_total = jnp.sum(rows_total[conv_taps + 2].reshape(heads_here, -1), axis=1)
    dt_bias_total = heads_total[0, :heads_here]
    a_log_total = heads_total[1, :heads_here]
    return (
        result,
        x_grad,
        norm_gain_total,
        w_z_share,
        w_x_share,
        w_bc_share,
        w_dt_share,
        conv_x_total,
        conv_x_bias_total,
        conv_bc_total,
        conv_bc_bias_total,
        dt_bias_total,
        a_log_total,
        d_skip_total,
        gate_norm_total,
        w_out_share,
    )


def solution(mesh):
    in_specs = (
        P("dp", None),
        P("dp", None),
        P(),
        P(None, "tensor"),
        P(None, "tensor"),
        P(),
        P(None, "tensor"),
        P(None, "tensor"),
        P("tensor"),
        P(),
        P(),
        P("tensor"),
        P("tensor"),
        P("tensor"),
        P("tensor"),
        P("tensor", None),
    )
    out_specs = (
        P("dp", "tensor"),
        P("dp", "tensor"),
        P("tensor"),
        P("dp", "tensor"),
        P("dp", "tensor"),
        P("dp", None),
        P("dp", "tensor"),
        P(None, "tensor"),
        P("tensor"),
        P(),
        P(),
        P("tensor"),
        P("tensor"),
        P("tensor"),
        P("tensor"),
        P("tensor", "dp"),
    )
    return jax.shard_map(
        on_device, mesh=mesh, in_specs=in_specs, out_specs=out_specs, check_vma=False
    )
```

```python
import functools

import jax
import jax.numpy as jnp
from jax import lax
from jax.experimental import pallas as pl
from jax.experimental.pallas import tpu as pltpu
from jax.sharding import PartitionSpec as P

GROUP = 256


epsilon = 1e-05
precise = lax.Precision.HIGHEST


def lead_contract(left, right):
    return lax.dot_general(
        left, right, (((0,), (0,)), ((), ())), preferred_element_type=jnp.float32
    )


def tail_contract(left, right):
    return lax.dot_general(
        left, right, (((1,), (1,)), ((), ())), preferred_element_type=jnp.float32
    )


def causal_conv(pre_conv, kernel, offset):
    taps = kernel.shape[0]
    padded = jnp.pad(pre_conv, ((taps - 1, 0), (0, 0)))
    summed = offset[None, :] + kernel[0][None, :] * padded[: pre_conv.shape[0]]
    for tap_index in range(1, taps):
        summed = (
            summed + kernel[tap_index][None, :] * padded[tap_index : tap_index + pre_conv.shape[0]]
        )
    return summed


LANES = 128


def low_dot(left, right, contract):
    return lax.dot_general(
        left.astype(jnp.bfloat16),
        right.astype(jnp.bfloat16),
        ((contract[0], contract[1]), ((), ())),
        preferred_element_type=jnp.float32,
    )


PLAIN, LEAD, TAIL = ((1,), (0,)), ((0,), (0,)), ((1,), (1,))


def shifted(rows, distance):
    if distance == 0:
        return rows
    length = rows.shape[0]
    at = lax.broadcasted_iota(jnp.int32, rows.shape, 0)
    moved = pltpu.roll(rows, distance % length, 0)
    keep = at >= distance if distance > 0 else at < length + distance
    return jnp.where(keep, moved, 0.0)


def conv_rows(pre, taps, offset):
    count = taps.shape[0]
    total = offset + taps[count - 1 : count] * pre
    for k in range(count - 1):
        total = total + taps[k : k + 1] * shifted(pre, count - 1 - k)
    return total


def pick(array, head):
    lane = lax.broadcasted_iota(jnp.int32, array.shape, 1)
    return jnp.sum(jnp.where(lane == head, array, 0.0), axis=1, keepdims=True)


def lower(size):
    return lax.broadcasted_iota(jnp.int32, (size, size), 0) >= lax.broadcasted_iota(
        jnp.int32, (size, size), 1
    )


def prepare(dt_ref, dtb_ref, alog_ref, bc_ref, cbc_ref, cbcb_ref, scratch):
    step_ref, run_ref, stept_ref, runt_ref, bc_low_ref, pair_ref = scratch
    step = dt_ref[...] + dtb_ref[...]
    step = jnp.maximum(step, 0.0) + jnp.log1p(jnp.exp(-jnp.abs(step)))
    step_ref[...] = step
    decay = step * -jnp.exp(alog_ref[...])
    u = conv_rows(bc_ref[...], cbc_ref[...], cbcb_ref[...])
    bc_low_ref[...] = (u * jax.nn.sigmoid(u)).astype(jnp.bfloat16)
    state = bc_low_ref.shape[1] // 2
    tri = lower(GROUP).astype(jnp.float32)
    for block in range(2):
        rows = slice(block * GROUP, (block + 1) * GROUP)
        run = jnp.dot(tri, decay[rows], precision=precise, preferred_element_type=jnp.float32)
        run_ref[rows, :] = run
        runt_ref[:, rows] = run.T
        stept_ref[:, rows] = step[rows].T
        pair_ref[block] = low_dot(bc_low_ref[rows, state:], bc_low_ref[rows, :state], TAIL)


def prepare_scratch(rows, width):
    return [
        pltpu.VMEM((rows, LANES), jnp.float32),
        pltpu.VMEM((rows, LANES), jnp.float32),
        pltpu.VMEM((LANES, rows), jnp.float32),
        pltpu.VMEM((LANES, rows), jnp.float32),
        pltpu.VMEM((rows, width), jnp.bfloat16),
        pltpu.VMEM((2, GROUP, GROUP), jnp.float32),
    ]


def forward_kernel(
    x_ref, cot_ref, gain_ref, wz_ref, wx_ref, wbc_ref, wdt_ref, cx_ref, cxb_ref, cbc_ref, cbcb_ref,
    dtb_ref, alog_ref, skip_ref, gnorm_ref, wout_ref,
    normed_ref, gate_ref, xpre_ref, bc_ref, dt_ref, mixed_ref, og_ref, state_ref, sums_ref,
    *scratch,
):
    step_ref, run_ref, stept_ref, runt_ref, bc_low_ref, pair_ref = scratch
    tokens = x_ref[...].astype(jnp.float32)
    inv_rms = lax.rsqrt(jnp.mean(tokens * tokens, axis=1, keepdims=True) + epsilon)
    normed_ref[...] = (tokens * inv_rms * gain_ref[...]).astype(jnp.bfloat16)
    bc_ref[...] = low_dot(normed_ref[...], wbc_ref[...], PLAIN)
    dt_ref[...] = low_dot(normed_ref[...], wdt_ref[...], PLAIN)
    prepare(dt_ref, dtb_ref, alog_ref, bc_ref, cbc_ref, cbcb_ref, scratch)
    sums_ref[...] = jnp.zeros_like(sums_ref)
    state = bc_low_ref.shape[1] // 2
    lane = lax.broadcasted_iota(jnp.int32, (1, LANES), 1)
    left = lane < LANES // 2

    def pair_step(p, carry):
        cols = pl.ds(pl.multiple_of(p * LANES, LANES), LANES)
        pre = low_dot(normed_ref[...], wx_ref[:, cols], PLAIN)
        xpre_ref[:, cols] = pre
        gate = low_dot(normed_ref[...], wz_ref[:, cols], PLAIN)
        gate_ref[:, cols] = gate
        u = conv_rows(pre, cx_ref[:, cols], cxb_ref[:, cols])
        x_low = (u * jax.nn.sigmoid(u)).astype(jnp.bfloat16)
        values = x_low.astype(jnp.float32)
        carried_state = None
        for block in range(2):
            rows = slice(block * GROUP, (block + 1) * GROUP)
            part = values[rows]
            b_rows, c_rows = bc_low_ref[rows, :state], bc_low_ref[rows, state:]
            run_cols = [pick(run_ref[rows, :], 2 * p + side) for side in range(2)]
            total = skip_ref[:, cols] * part
            for side in range(2):
                run_row = runt_ref[pl.ds(2 * p + side, 1), rows]
                step_row = stept_ref[pl.ds(2 * p + side, 1), rows]
                differ = jnp.where(lower(GROUP), run_cols[side] - run_row, -jnp.inf)
                weights = pair_ref[block] * jnp.exp(differ) * step_row
                mine = left if side == 0 else ~left
                total = total + low_dot(weights, jnp.where(mine, part, 0.0), PLAIN)
            run = jnp.where(left, run_cols[0], run_cols[1])
            if block == 0:
                step = jnp.where(
                    left, pick(step_ref[rows, :], 2 * p), pick(step_ref[rows, :], 2 * p + 1)
                )
                to_end = jnp.exp(run[GROUP - 1 :] - run) * step
                carried_state = low_dot(to_end * part, b_rows, LEAD)
                state_ref[cols, :] = carried_state
            else:
                total = total + jnp.exp(run) * low_dot(c_rows, carried_state, TAIL)
            mixed_ref[rows, cols] = total
        gated = mixed_ref[:, cols] * gate * jax.nn.sigmoid(gate)
        og = low_dot(cot_ref[...], wout_ref[cols, :], TAIL)
        og_ref[:, cols] = og
        square = jnp.sum(gated * gated, axis=1, keepdims=True)
        inner = jnp.sum(og * gnorm_ref[:, cols] * gated, axis=1, keepdims=True)
        sums_ref[...] += jnp.where(lane == 0, square, 0.0) + jnp.where(lane == 1, inner, 0.0)
        return carry

    lax.fori_loop(0, gate_ref.shape[1] // LANES, pair_step, 0)


def backward_kernel(
    total_width,
    sums_ref, gate_ref, xpre_ref, bc_ref, dt_ref, mixed_ref, og_ref, state_ref,
    wz_ref, wx_ref, wdt_ref, cx_ref, cxb_ref, cbc_ref, cbcb_ref, dtb_ref, alog_ref, skip_ref,
    gnorm_ref, wout_ref,
    gout_ref, y_ref, glow_ref, xlow_ref, dtlow_ref, bcg_ref, partial_ref, rows_ref, heads_ref,
    *scratch,
):
    step_ref, run_ref, stept_ref, runt_ref, bc_low_ref, pair_ref = scratch[:6]
    run_grad_ref, direct_ref, colt_ref, both_ref = scratch[6:]
    prepare(dt_ref, dtb_ref, alog_ref, bc_ref, cbc_ref, cbcb_ref, scratch[:6])
    for ref in (run_grad_ref, direct_ref, colt_ref, both_ref, bcg_ref, rows_ref, heads_ref):
        ref[...] = jnp.zeros_like(ref)
    state = bc_low_ref.shape[1] // 2
    lane = lax.broadcasted_iota(jnp.int32, (1, LANES), 1)
    left = lane < LANES // 2
    taps = cx_ref.shape[0]

    def split_sum(array):
        return (
            jnp.sum(jnp.where(left, array, 0.0), axis=1, keepdims=True),
            jnp.sum(jnp.where(left, 0.0, array), axis=1, keepdims=True),
        )

    def pair_step(p, carry):
        cols = pl.ds(pl.multiple_of(p * LANES, LANES), LANES)
        spread = lax.rsqrt(sums_ref[:, 0:1] / total_width + epsilon)
        row_dot = sums_ref[:, 1:2]
        gate, mixed, og = gate_ref[:, cols], mixed_ref[:, cols], og_ref[:, cols]
        sigma = jax.nn.sigmoid(gate)
        gate_act = gate * sigma
        gated = mixed * gate_act
        gout_ref[:, cols] = (gated * spread * gnorm_ref[:, cols]).astype(jnp.bfloat16)
        rows_ref[5:6, cols] = jnp.sum(og * gated * spread, axis=0, keepdims=True)
        gated_grad = spread * og * gnorm_ref[:, cols] - gated * (
            spread * spread * spread * row_dot / total_width
        )
        grad = gated_grad * gate_act
        glow_ref[:, cols] = (
            gated_grad * mixed * sigma * (1.0 + gate * (1.0 - sigma))
        ).astype(jnp.bfloat16)
        pre = xpre_ref[:, cols]
        u = conv_rows(pre, cx_ref[:, cols], cxb_ref[:, cols])
        act = jax.nn.sigmoid(u)
        values = (u * act).astype(jnp.bfloat16).astype(jnp.float32)
        rows_ref[6:7, cols] = jnp.sum(grad * values, axis=0, keepdims=True)
        kept = state_ref[cols, :]
        later = None
        pieces = [None, None]
        for block in (1, 0):
            rows = slice(block * GROUP, (block + 1) * GROUP)
            part, dy = values[rows], grad[rows]
            b_rows, c_rows = bc_low_ref[rows, :state], bc_low_ref[rows, state:]
            run_cols = [pick(run_ref[rows, :], 2 * p + side) for side in range(2)]
            run = jnp.where(left, run_cols[0], run_cols[1])
            total = skip_ref[:, cols] * dy
            run_parts, direct_parts = [], [0.0, 0.0]
            for side in range(2):
                run_row = runt_ref[pl.ds(2 * p + side, 1), rows]
                step_row = stept_ref[pl.ds(2 * p + side, 1), rows]
                decay = jnp.exp(jnp.where(lower(GROUP), run_cols[side] - run_row, -jnp.inf))
                mine = left if side == 0 else ~left
                dy_mine = jnp.where(mine, dy, 0.0)
                near = low_dot(dy_mine, part, TAIL) * decay
                direct = near * pair_ref[block]
                both_ref[block] += near * step_row
                colt_ref[pl.ds(2 * p + side, 1), rows] = jnp.sum(direct, axis=0, keepdims=True)
                run_parts.append(jnp.sum(direct * step_row, axis=1, keepdims=True))
                total = total + low_dot(pair_ref[block] * decay * step_row, dy_mine, LEAD)
            if block == 1:
                grown = jnp.exp(run) * dy
                extra = split_sum(grown * low_dot(c_rows, kept, TAIL))
                bcg_ref[rows, state:] += low_dot(grown, kept, PLAIN)
                later = low_dot(grown, c_rows, LEAD)
                run_parts = [run_parts[side] + extra[side] for side in range(2)]
            else:
                step = jnp.where(
                    left, pick(step_ref[rows, :], 2 * p), pick(step_ref[rows, :], 2 * p + 1)
                )
                fall = jnp.exp(run[GROUP - 1 :] - run)
                to_end = fall * step
                back = low_dot(b_rows, later, TAIL)
                total = total + to_end * back
                direct_parts = split_sum(fall * part * back)
                extra = split_sum(to_end * part * back)
                bcg_ref[rows, :state] += low_dot(to_end * part, later, PLAIN)
                last = lax.broadcasted_iota(jnp.int32, (GROUP, 1), 0) == GROUP - 1
                run_parts = [
                    run_parts[side]
                    - extra[side]
                    + jnp.where(last, jnp.sum(extra[side], axis=0, keepdims=True), 0.0)
                    for side in range(2)
                ]
                direct_ref[rows, :] += jnp.where(
                    lane == 2 * p, direct_parts[0], 0.0
                ) + jnp.where(lane == 2 * p + 1, direct_parts[1], 0.0)
            run_grad_ref[rows, :] += jnp.where(lane == 2 * p, run_parts[0], 0.0) + jnp.where(
                lane == 2 * p + 1, run_parts[1], 0.0
            )
            pieces[block] = total
        du = jnp.concatenate(pieces, axis=0) * act * (1.0 + u * (1.0 - act))
        rows_ref[4:5, cols] = jnp.sum(du, axis=0, keepdims=True)
        back = 0.0
        for k in range(taps):
            rows_ref[k : k + 1, cols] = jnp.sum(
                du * shifted(pre, taps - 1 - k), axis=0, keepdims=True
            )
            back = back + cx_ref[k : k + 1, cols] * shifted(du, k - taps + 1)
        xlow_ref[:, cols] = back.astype(jnp.bfloat16)
        return carry

    lax.fori_loop(0, gate_ref.shape[1] // LANES, pair_step, 0)
    rate = -jnp.exp(alog_ref[...])
    upper = lower(GROUP).astype(jnp.float32)
    for block in range(2):
        rows = slice(block * GROUP, (block + 1) * GROUP)
        b_rows, c_rows = bc_low_ref[rows, :state], bc_low_ref[rows, state:]
        bcg_ref[rows, :state] += low_dot(both_ref[block], c_rows, LEAD)
        bcg_ref[rows, state:] += low_dot(both_ref[block], b_rows, PLAIN)
        direct = colt_ref[:, rows].T
        step = step_ref[rows, :]
        run_grad = run_grad_ref[rows, :] - direct * step
        suffix = lax.dot_general(
            upper, run_grad, (LEAD, ((), ())), precision=precise, preferred_element_type=jnp.float32
        )
        sig = jax.nn.sigmoid(dt_ref[rows, :] + dtb_ref[...])
        dt_grad = (direct_ref[rows, :] + direct + rate * suffix) * sig
        dtlow_ref[rows, :] = dt_grad.astype(jnp.bfloat16)
        heads_ref[0:1, :] += jnp.sum(dt_grad, axis=0, keepdims=True)
        heads_ref[1:2, :] += rate * jnp.sum(step * suffix, axis=0, keepdims=True)
    y_ref[...] = low_dot(gout_ref[...], wout_ref[...], PLAIN)
    partial_ref[...] = (
        low_dot(glow_ref[...], wz_ref[...], TAIL)
        + low_dot(xlow_ref[...], wx_ref[...], TAIL)
        + low_dot(dtlow_ref[...], wdt_ref[...], TAIL)
    )


def local_call(body, name, outs, scratch, *operands):
    vmem = pl.BlockSpec(memory_space=pltpu.VMEM)
    return pl.pallas_call(
        body,
        out_shape=tuple(jax.ShapeDtypeStruct(shape, kind) for shape, kind in outs),
        in_specs=[vmem] * len(operands),
        out_specs=(vmem,) * len(outs),
        scratch_shapes=scratch,
        compiler_params=pltpu.CompilerParams(vmem_limit_bytes=44 * 2**20),
        name=name,
    )(*operands)


PACK_ROWS = 16


def bit_orders(levels):
    if levels == 4:
        return ((0, 1, 2, 3), (1, 0, 2, 3), (2, 3, 0, 1), (0, 1, 2, 3))
    base = tuple(range(levels))
    third = max(1, levels // 3)
    return (base, base[third:] + base[:third], base[2 * third :] + base[: 2 * third], base)


def reduce_kernel(
    orders, a_ref, b_ref, c_ref, d_ref, pack_ref,
    oa_ref, ob_ref, oc_ref, od_ref, obc_ref, opack_ref,
    ra_ref, rb_ref, rc_ref, rd_ref, rpack_ref, spack_ref, send_sem, recv_sem, psend_sem, precv_sem,
):
    parts, outs = (a_ref, b_ref, c_ref, d_ref), (oa_ref, ob_ref, oc_ref, od_ref)
    lands = (ra_ref, rb_ref, rc_ref, rd_ref)
    groups = range(len(parts))
    levels = len(orders[0])
    count = 2**levels
    sizes = [count // 2 ** (stage + 1) for stage in range(levels)]
    starts = [sum(sizes[:stage]) for stage in range(levels)]
    me = lax.axis_index("dp")

    def my_bit(bit):
        return (me // 2**bit) % 2

    def partner(bit):
        return me + (1 - 2 * my_bit(bit)) * 2**bit

    def first_chunk(order, k, kept):
        own = my_bit(order[0])
        chunk = (own if kept else 1 - own) * 2 ** order[0]
        for place in range(1, levels):
            relative = (k // 2 ** (levels - 1 - place)) % 2
            chunk = chunk + ((my_bit(order[place]) + relative + 1) % 2) * 2 ** order[place]
        return chunk

    def transfer(g, stage, k):
        if stage == 0:
            source = parts[g].at[first_chunk(orders[g], k, False)]
        else:
            source = lands[g].at[starts[stage - 1] + k]
        slot = starts[stage] + k
        return pltpu.make_async_remote_copy(
            src_ref=source,
            dst_ref=lands[g].at[slot],
            send_sem=send_sem.at[g, slot],
            recv_sem=recv_sem.at[g, slot],
            device_id={"dp": partner(orders[g][stage])},
            device_id_type=pl.DeviceIdType.MESH,
        )

    def pack_transfer(stage):
        return pltpu.make_async_remote_copy(
            src_ref=pack_ref if stage == 0 else spack_ref.at[stage - 1],
            dst_ref=rpack_ref.at[stage],
            send_sem=psend_sem.at[stage],
            recv_sem=precv_sem.at[stage],
            device_id={"dp": partner(stage)},
            device_id_type=pl.DeviceIdType.MESH,
        )

    barrier = pltpu.get_barrier_semaphore()
    for bit in range(levels):
        pl.semaphore_signal(
            barrier, inc=1, device_id={"dp": partner(bit)}, device_id_type=pl.DeviceIdType.MESH
        )
    pl.semaphore_wait(barrier, levels)

    def begin(k, carry):
        for g in groups:
            transfer(g, 0, k).start()
        return carry

    pack_transfer(0).start()
    lax.fori_loop(0, sizes[0], begin, 0)
    for stage in range(levels):
        half = sizes[stage] // 2

        def step(k, carry, stage=stage, forward=False):
            for g in groups:
                transfer(g, stage, k).wait_recv()
                slot = starts[stage] + k
                if stage == 0:
                    own = parts[g][first_chunk(orders[g], k, True)]
                else:
                    own = lands[g][starts[stage - 1] + sizes[stage] + k]
                total = lands[g][slot] + own
                if stage < levels - 1:
                    lands[g][slot] = total
                else:
                    main = outs[g].shape[1]
                    outs[g][...] = total[:, :main]
                    extra = total.shape[1] - main
                    if extra:
                        obc_ref[:, (g - 1) * extra : g * extra] = total[:, main:]
                if forward:
                    transfer(g, stage + 1, k).start()
            return carry

        if stage < levels - 1:
            lax.fori_loop(0, half, functools.partial(step, forward=True), 0)
            lax.fori_loop(half, sizes[stage], step, 0)
        else:
            step(0, 0)
        pack_transfer(stage).wait_recv()
        before = pack_ref[...] if stage == 0 else spack_ref[stage - 1]
        pack_total = before + rpack_ref[stage]
        if stage == levels - 1:
            opack_ref[...] = pack_total
        else:
            spack_ref[stage] = pack_total
            pack_transfer(stage + 1).start()
    for stage in range(levels):
        pack_transfer(stage).wait_send()

        def finish(k, carry, stage=stage):
            for g in groups:
                transfer(g, stage, k).wait_send()
            return carry

        lax.fori_loop(0, sizes[stage], finish, 0)


def reduce_all(a, b, c, d, pack):
    count, rows, width = a.shape
    levels = count.bit_length() - 1
    vmem = pl.BlockSpec(memory_space=pltpu.VMEM)
    widths = (width, width, width, d.shape[2], 2 * (b.shape[2] - width))
    return pl.pallas_call(
        functools.partial(reduce_kernel, bit_orders(levels)),
        out_shape=tuple(jax.ShapeDtypeStruct((rows, size), jnp.float32) for size in widths)
        + (jax.ShapeDtypeStruct(pack.shape, jnp.float32),),
        in_specs=[vmem] * 5,
        out_specs=(vmem,) * 6,
        scratch_shapes=[
            pltpu.VMEM((count - 1, rows, part.shape[2]), jnp.float32) for part in (a, b, c, d)
        ]
        + [
            pltpu.VMEM((levels,) + pack.shape, jnp.float32),
            pltpu.VMEM((levels,) + pack.shape, jnp.float32),
            pltpu.SemaphoreType.DMA((4, count - 1)),
            pltpu.SemaphoreType.DMA((4, count - 1)),
            pltpu.SemaphoreType.DMA((levels,)),
            pltpu.SemaphoreType.DMA((levels,)),
        ],
        compiler_params=pltpu.CompilerParams(
            collective_id=0, has_side_effects=True, vmem_limit_bytes=44 * 2**20
        ),
        name="reduce_all",
    )(a, b, c, d, pack)


def pair_kernel(halved, *refs):
    count = len(halved)
    sources, outs, lands = refs[:count], refs[count : 2 * count], refs[2 * count : 3 * count]
    send_sem, recv_sem = refs[3 * count :]
    me = lax.axis_index("tensor")
    other = 1 - me

    def view(i, owner):
        if not halved[i]:
            return sources[i]
        width = outs[i].shape[1]
        return sources[i].at[:, pl.ds(pl.multiple_of(owner * width, LANES), width)]

    barrier = pltpu.get_barrier_semaphore()
    pl.semaphore_signal(
        barrier, inc=1, device_id={"tensor": other}, device_id_type=pl.DeviceIdType.MESH
    )
    pl.semaphore_wait(barrier, 1)
    copies = [
        pltpu.make_async_remote_copy(
            src_ref=view(i, other),
            dst_ref=lands[i],
            send_sem=send_sem.at[i],
            recv_sem=recv_sem.at[i],
            device_id={"tensor": other},
            device_id_type=pl.DeviceIdType.MESH,
        )
        for i in range(count)
    ]
    for copy in copies:
        copy.start()
    for i in range(count):
        copies[i].wait_recv()
        outs[i][...] = view(i, me)[...] + lands[i][...]
    for copy in copies:
        copy.wait_send()


def pair_sum(arrays, halved, number):
    vmem = pl.BlockSpec(memory_space=pltpu.VMEM)
    shapes = [
        (array.shape[0], array.shape[1] // 2 if half else array.shape[1])
        for array, half in zip(arrays, halved)
    ]
    return pl.pallas_call(
        functools.partial(pair_kernel, halved),
        out_shape=tuple(jax.ShapeDtypeStruct(shape, jnp.float32) for shape in shapes),
        in_specs=[vmem] * len(arrays),
        out_specs=(vmem,) * len(arrays),
        scratch_shapes=[pltpu.VMEM(shape, jnp.float32) for shape in shapes]
        + [pltpu.SemaphoreType.DMA((len(arrays),))] * 2,
        compiler_params=pltpu.CompilerParams(
            collective_id=number, has_side_effects=True, vmem_limit_bytes=24 * 2**20
        ),
        name="pair_sum",
    )(*arrays)


def on_device(
    x_in,
    cotangent,
    norm_gain,
    w_z,
    w_x,
    w_bc,
    w_dt,
    conv_x,
    conv_x_bias,
    conv_bc,
    conv_bc_bias,
    dt_bias,
    a_log,
    d_skip,
    gate_norm,
    w_out,
):
    row_count, model_width = x_in.shape
    pair_count = lax.axis_size("tensor")
    half_width = model_width // pair_count
    col_start = lax.axis_index("tensor") * half_width
    inner_width = w_z.shape[1]
    heads_here = dt_bias.shape[0]
    total_width = inner_width * pair_count
    tokens = x_in.astype(jnp.float32)
    inv_rms = lax.rsqrt(jnp.mean(tokens * tokens, axis=1, keepdims=True) + epsilon)
    x_hat = tokens * inv_rms
    bc_width = w_bc.shape[1]

    def head_row(vector):
        return jnp.pad(vector, (0, LANES - heads_here))[None, :]

    w_dt_padded = jnp.pad(w_dt, ((0, 0), (0, LANES - heads_here)))
    skip_row = jnp.repeat(d_skip, inner_width // heads_here)[None, :]
    wide = (row_count, inner_width)
    shared = (
        conv_x,
        conv_x_bias[None, :],
        conv_bc,
        conv_bc_bias[None, :],
        head_row(dt_bias),
        head_row(a_log),
        skip_row,
        gate_norm[None, :],
        w_out,
    )
    normed, gate_pre, x_pre, bc_pre, dt_pre, mixed_out, out_grad, states, sums = local_call(
        forward_kernel,
        "forward",
        (
            ((row_count, model_width), jnp.bfloat16),
            (wide, jnp.float32),
            (wide, jnp.float32),
            ((row_count, bc_width), jnp.float32),
            ((row_count, LANES), jnp.float32),
            (wide, jnp.float32),
            (wide, jnp.float32),
            ((inner_width, bc_width // 2), jnp.float32),
            ((row_count, LANES), jnp.float32),
        ),
        prepare_scratch(row_count, bc_width),
        x_in, cotangent, norm_gain[None, :], w_z, w_x, w_bc, w_dt_padded, *shared,
    )
    (sums,) = pair_sum((sums,), (False,), 1)
    gate_out, y_part, gate_low, x_pre_low, dt_padded, bc_part_grad, partial_grad, rows, heads = (
        local_call(
            functools.partial(backward_kernel, total_width),
            "backward",
            (
                (wide, jnp.bfloat16),
                ((row_count, model_width), jnp.float32),
                (wide, jnp.bfloat16),
                (wide, jnp.bfloat16),
                ((row_count, LANES), jnp.bfloat16),
                ((row_count, bc_width), jnp.float32),
                ((row_count, model_width), jnp.float32),
                ((8, inner_width), jnp.float32),
                ((8, LANES), jnp.float32),
            ),
            prepare_scratch(row_count, bc_width)
            + [
                pltpu.VMEM((row_count, LANES), jnp.float32),
                pltpu.VMEM((row_count, LANES), jnp.float32),
                pltpu.VMEM((LANES, row_count), jnp.float32),
                pltpu.VMEM((2, GROUP, GROUP), jnp.float32),
            ],
            sums, gate_pre, x_pre, bc_pre, dt_pre, mixed_out, out_grad, states,
            w_z, w_x, w_dt_padded, *shared,
        )
    )
    bc_conv_grad, partial_total, out_share = pair_sum(
        (bc_part_grad, partial_grad, y_part), (False, False, True), 2
    )
    token_half = lax.dynamic_slice_in_dim(tokens, col_start, half_width, 1)
    result = (token_half + out_share).astype(jnp.bfloat16)
    w_out_grad = lead_contract(cotangent, gate_out)
    bc_conv_back = jax.vjp(
        lambda *pieces: jax.nn.silu(causal_conv(*pieces)), bc_pre, conv_bc, conv_bc_bias
    )[1]
    bc_pre_grad, conv_bc_grad, conv_bc_bias_grad = bc_conv_back(bc_conv_grad)
    bc_pre_low = bc_pre_grad.astype(jnp.bfloat16)
    conv_taps = conv_x.shape[0]
    hat_half = lax.dynamic_slice_in_dim(x_hat, col_start, half_width, 1)
    gain_half = lax.dynamic_slice_in_dim(norm_gain, col_start, half_width, 0)
    normed_grad = partial_total + tail_contract(bc_pre_low, w_bc)
    grad_half = lax.dynamic_slice_in_dim(normed_grad, col_start, half_width, 1)
    weighted_in = grad_half * gain_half[None, :]
    in_dot = jnp.sum(normed_grad * norm_gain[None, :] * x_hat, axis=1)
    norm_gain_grad = jnp.sum(grad_half * hat_half, axis=0)
    cot_half = lax.dynamic_slice_in_dim(cotangent, col_start, half_width, 1).astype(jnp.float32)
    x_grad = (cot_half + inv_rms * (weighted_in - hat_half * in_dot[:, None] / model_width)).astype(
        jnp.bfloat16
    )
    count = lax.axis_size("dp")
    half_bc = bc_pre_low.shape[1] // 2

    def chunks(array):
        return array.reshape(count, model_width // count, array.shape[1])

    part_a = chunks(w_out_grad)
    part_d = chunks(lead_contract(normed, dt_padded))
    part_b = chunks(
        lead_contract(normed, jnp.concatenate([gate_low, bc_pre_low[:, :half_bc]], axis=1))
    )
    part_c = chunks(
        lead_contract(normed, jnp.concatenate([x_pre_low, bc_pre_low[:, half_bc:]], axis=1))
    )
    small = (
        rows,
        conv_bc_grad,
        conv_bc_bias_grad,
        heads[:2],
        norm_gain_grad,
    )
    flat = jnp.concatenate([array.reshape(-1) for array in small])
    pack = jnp.pad(flat, (0, PACK_ROWS * 768 - flat.shape[0])).reshape(PACK_ROWS, 768)
    sum_a, w_z_share, w_x_share, sum_d, w_bc_share, pack_total = reduce_all(
        part_a, part_b, part_c, part_d, pack
    )
    w_out_share = jnp.transpose(sum_a)
    w_dt_share = sum_d[:, :heads_here]
    flat_total = pack_total.reshape(-1)
    totals, at = [], 0
    for array in small:
        totals.append(flat_total[at : at + array.size].reshape(array.shape))
        at += array.size
    rows_total, conv_bc_total, conv_bc_bias_total, heads_total, norm_gain_total = totals
    conv_x_total = rows_total[:conv_taps]
    conv_x_bias_total = rows_total[conv_taps]
    gate_norm_total = rows_total[conv_taps + 1]
    d_skip_total = jnp.sum(rows_total[conv_taps + 2].reshape(heads_here, -1), axis=1)
    dt_bias_total = heads_total[0, :heads_here]
    a_log_total = heads_total[1, :heads_here]
    return (
        result,
        x_grad,
        norm_gain_total,
        w_z_share,
        w_x_share,
        w_bc_share,
        w_dt_share,
        conv_x_total,
        conv_x_bias_total,
        conv_bc_total,
        conv_bc_bias_total,
        dt_bias_total,
        a_log_total,
        d_skip_total,
        gate_norm_total,
        w_out_share,
    )


def solution(mesh):
    in_specs = (
        P("dp", None),
        P("dp", None),
        P(),
        P(None, "tensor"),
        P(None, "tensor"),
        P(),
        P(None, "tensor"),
        P(None, "tensor"),
        P("tensor"),
        P(),
        P(),
        P("tensor"),
        P("tensor"),
        P("tensor"),
        P("tensor"),
        P("tensor", None),
    )
    out_specs = (
        P("dp", "tensor"),
        P("dp", "tensor"),
        P("tensor"),
        P("dp", "tensor"),
        P("dp", "tensor"),
        P("dp", None),
        P("dp", "tensor"),
        P(None, "tensor"),
        P("tensor"),
        P(),
        P(),
        P("tensor"),
        P("tensor"),
        P("tensor"),
        P("tensor"),
        P("tensor", "dp"),
    )
    return jax.shard_map(
        on_device, mesh=mesh, in_specs=in_specs, out_specs=out_specs, check_vma=False
    )
```
